1024 devices in a mesh: replica: 16 (over y, core), owner: 64 (over z, x).
Axes of the slice: x: 4, y: 8, z: 16, core: 2. Of those that a mesh axis runs over, the one named last changes fastest.
Arguments:
- grad_parts: bfloat16 [16, 144, 512, 512], P('replica', None, 'owner'), may hold values from -0.29882812 to 0.29882812
- owner_of: int32 [144, 1], replicated, may hold values from 0 to 63; in each aligned block of 144 rows (0 to 143, 144 to 287, ...) at most 5 rows name the same one
- stats_left: bfloat16 [64, 5, 512, 512], P('owner', None, 'replica'), may hold values from -6 to 6
- stats_right: bfloat16 [64, 5, 512, 512], P('owner', None, 'replica'), may hold values from -6 to 6
- basis_left: bfloat16 [64, 5, 512, 512], P('owner'), may hold values from -0.25 to 0.25
- basis_right: bfloat16 [64, 5, 512, 512], P('owner'), may hold values from -0.25 to 0.25
- moment_first: float32 [64, 5, 512, 512], P('owner', None, 'replica'), may hold values from -0.6 to 0.6
- moment_second: float32 [64, 5, 512, 512], P('owner', None, 'replica'), may hold values from 0.01 to 0.04
Outputs:
- new_left: bfloat16 [64, 5, 512, 512], P('owner', None, 'replica')
- new_right: bfloat16 [64, 5, 512, 512], P('owner', None, 'replica')
- new_first: float32 [64, 5, 512, 512], P('owner', None, 'replica')
- new_second: float32 [64, 5, 512, 512], P('owner', None, 'replica')
- update: bfloat16 [144, 512, 512], P(None, 'owner', 'replica')
The draws below stay inside these ranges and needn't reach their ends.
Inputs may be any that keep to these rules, and one draw needn't show every extreme that they name: owner_of[b, 0] is the owner of block b; every owner is named, none by more than 5 blocks, and one by exactly 5.
All inputs are finite; a program needn't handle non-finite values.
Results may differ from the reference program's by a relative error of at most 0.02.
Values may be sent and summed in bfloat16 or wider, within the bound.
A program may use at most 32 MiB of HBM per device.

```python
import math
import jax
import jax.numpy as jnp
import numpy as np
from jax import lax

BLOCK = 512
BLOCKS = 144
CAPACITY = 5
N_REPLICA = 16
N_OWNER = 64


def spiked(entries, stream_key, source, target, shards_of, factor):
    def block_of(dim):
        return (jnp.arange(entries.shape[dim]) // (entries.shape[dim] // shards_of)).reshape((-1,) + (1,) * (entries.ndim - 1 - dim))

    one_side = jax.random.permutation(stream_key, shards_of)[block_of(target)]
    second = (block_of(target) + shards_of // 2) % shards_of
    return jnp.where((block_of(source) == one_side) | (block_of(source) == second), factor * entries, entries)


def block_scale(stream_key, extent, pieces, smallest, high):
    loudness, own = 1.0, jax.random.fold_in(stream_key, 6)
    for axis_at, parts in pieces:
        heights = jnp.exp(jax.random.uniform(jax.random.fold_in(own, axis_at), (parts,), jnp.float32, smallest / len(pieces), high / len(pieces)))
        loudness = loudness * jnp.repeat(heights, extent[axis_at] // parts).reshape([-1 if axis == axis_at else 1 for axis in range(len(extent))])
    return loudness


def shared_out(own_key, own, number, rows, number_of, top, reach, lean):
    sequence = jax.random.permutation(own_key, number_of)
    heavy_load, ordinary = load_shares(number_of, rows * top, reach, lean, True), load_shares(number_of, rows * top, reach, lean, False)
    places = jnp.arange(number_of)

    def named(sizes, offset_by):
        used = int((sizes > 0).sum())
        fixed = max(1, used // 4)
        passed = fixed + (places - fixed + offset_by * (used - fixed)) % max(1, number_of - fixed)
        return jnp.zeros((number_of,), jnp.int32).at[sequence[jnp.where(places < fixed, places, passed)]].set(jnp.asarray(sizes, jnp.int32))

    sizes = jnp.where(number % 4 == 0, named(heavy_load, number // 4), named(ordinary, number - number // 4 - 1))
    mixed = jax.random.permutation(jax.random.fold_in(own, 3), number_of)
    giver, taker = mixed[0:number_of // 2 * 2:2], mixed[1:number_of // 2 * 2:2]
    room = jnp.minimum(sizes[giver] - 1, reach - sizes[taker]) // 2
    room = jnp.where((giver == sequence[0]) | (taker == sequence[0]) | (sizes[taker] == 0), 0, jnp.maximum(room, 0))
    passed = jax.random.randint(jax.random.fold_in(own, 4), (number_of // 2,), 0, 1 << 20) % (room + 1)
    sizes = sizes.at[giver].add(-passed).at[taker].add(passed)
    labels = jnp.searchsorted(jnp.cumsum(sizes), jnp.arange(rows * top), side="right").astype(jnp.int32)
    listing = labels.reshape(top, rows).T
    listing = listing[jax.random.permutation(jax.random.fold_in(own, 1), rows)]
    offset_by = jax.random.randint(jax.random.fold_in(own, 2), (rows, 1), 0, top)
    return jnp.take_along_axis(listing, (jnp.arange(top)[None, :] + offset_by) % top, axis=1)


def load_shares(count, total, reach, lean, full):
    weights = [(1 << 20) // math.isqrt(grade ** lean) + 1 for grade in range(1, count + 1)]
    largest = reach if full else min(reach, max(-(-total // count), total * weights[0] // sum(weights)))
    least = 1 if total - largest >= count - 1 else 0
    holding, surplus = [largest] + [least] * (count - 1), total - largest - least * (count - 1)
    while surplus > 0:
        candidates = [i for i in range(1, count) if holding[i] < largest] or [i for i in range(1, count) if holding[i] < reach]
        mass, left = sum([weights[i] for i in candidates]), surplus
        for i in candidates:
            addition = min(reach - holding[i], max(1, left * weights[i] // mass), surplus)
            holding[i] = holding[i] + addition
            surplus = surplus - addition
    return np.array(holding)


def noise(key, shape, width, most, cuts=(), held_as=jnp.bfloat16):
    values = width * jax.random.normal(key, shape, jnp.float32)
    if cuts:
        values = values * block_scale(key, shape, cuts, -0.22, 0.18)
    return jnp.clip(values, -most, most).astype(held_as)


def gaussian_with(stream_key, shape, width, limit, pieces, heavy, kind=jnp.bfloat16):
    values = width * jax.random.normal(stream_key, shape, jnp.float32)
    if pieces:
        values = values * block_scale(stream_key, shape, pieces, -0.22, 0.18)
    return jnp.clip(spiked(values, jax.random.fold_in(stream_key, 3), *heavy), -limit, limit).astype(kind)


def setup_inputs(seed: int = 0) -> dict:
    key_list = jax.random.split(jax.random.key(seed), 9)
    grad_parts = gaussian_with(key_list[0], (N_REPLICA, BLOCKS, BLOCK, BLOCK), 0.05, 0.29882812, ((0, 16), (2, 64)), (0, 3, 16, 2.0))
    owner_of_keys = jax.random.split(jax.random.fold_in(key_list[1], 1), BLOCKS // BLOCKS)
    owner_of_turns = jax.random.permutation(jax.random.fold_in(key_list[1], 3), BLOCKS // BLOCKS)
    owner_of = jax.vmap(lambda own, number: shared_out(jax.random.fold_in(key_list[1], 2), own, number, BLOCKS, N_OWNER, 1, CAPACITY, 2))(owner_of_keys, owner_of_turns).reshape((BLOCKS, 1))
    stats_left = noise(key_list[2], (N_OWNER, CAPACITY, BLOCK, BLOCK), 1.0, 6.0, ((0, 64), (2, 16)))
    stats_right = noise(key_list[3], (N_OWNER, CAPACITY, BLOCK, BLOCK), 1.0, 6.0, ((0, 64), (2, 16)))
    basis_left = noise(key_list[4], (N_OWNER, CAPACITY, BLOCK, BLOCK), BLOCK ** -0.5, 0.25, ((0, 64),))
    basis_right = noise(key_list[5], (N_OWNER, CAPACITY, BLOCK, BLOCK), BLOCK ** -0.5, 0.25, ((0, 64),))
    moment_first = noise(key_list[6], (N_OWNER, CAPACITY, BLOCK, BLOCK), 0.1, 0.6, ((0, 64), (2, 16)), jnp.float32)
    moment_second = jnp.clip(jnp.exp(math.log(0.04) - 1.3862944 * jax.random.uniform(key_list[7], (N_OWNER, CAPACITY, BLOCK, BLOCK), jnp.float32) ** block_scale(key_list[7], (N_OWNER, CAPACITY, BLOCK, BLOCK), ((0, 64), (2, 16)), -0.2, 0.2)), 0.01, 0.04)
    return dict(grad_parts=grad_parts, owner_of=owner_of, stats_left=stats_left, stats_right=stats_right, basis_left=basis_left, basis_right=basis_right, moment_first=moment_first, moment_second=moment_second)


BETA_FIRST = 0.9
BETA_SECOND = 0.95
EPSILON = 1e-08

def slot_places(owner_of):
    owners = owner_of[:, 0].astype(jnp.int32)
    onehot = (owners[:, None] == jnp.arange(N_OWNER, dtype=jnp.int32)[None, :]).astype(jnp.int32)
    before = (jnp.cumsum(onehot, axis=0) - onehot).astype(jnp.int32)
    slot_rank = lax.optimization_barrier(jnp.sum(before * onehot, axis=1)).astype(jnp.int32)
    return (owners, slot_rank)

def one_slot(slot_items):
    grad_block, left_stat, right_stat, left_basis, right_basis, first_old, second_old = slot_items
    left_new = (BETA_SECOND * left_stat.astype(jnp.float32) + (1.0 - BETA_SECOND) * jnp.dot(grad_block, grad_block.T, preferred_element_type=jnp.float32)).astype(jnp.bfloat16)
    right_new = (BETA_SECOND * right_stat.astype(jnp.float32) + (1.0 - BETA_SECOND) * jnp.dot(grad_block.T, grad_block, preferred_element_type=jnp.float32)).astype(jnp.bfloat16)
    half_rot = jnp.dot(left_basis.T, grad_block, preferred_element_type=jnp.float32).astype(jnp.bfloat16)
    rotated = jnp.dot(half_rot, right_basis, preferred_element_type=jnp.float32)
    first_new = BETA_FIRST * first_old + (1.0 - BETA_FIRST) * rotated
    second_new = BETA_SECOND * second_old + (1.0 - BETA_SECOND) * rotated * rotated
    direction = (first_new / (jnp.sqrt(second_new) + EPSILON)).astype(jnp.bfloat16)
    back_half = jnp.dot(direction, right_basis.T, preferred_element_type=jnp.float32).astype(jnp.bfloat16)
    update_block = jnp.dot(left_basis, back_half, preferred_element_type=jnp.float32).astype(jnp.bfloat16)
    return (left_new, right_new, first_new, second_new, update_block)

def flatten_slots(array):
    return array.reshape((N_OWNER * CAPACITY,) + array.shape[2:])

def reference(grad_parts, owner_of, stats_left, stats_right, basis_left, basis_right, moment_first, moment_second):

    def accumulate(running, one_part):
        return (running + one_part.astype(jnp.float32), None)
    grad_sum, _ = lax.scan(accumulate, jnp.zeros(grad_parts.shape[1:], jnp.float32), grad_parts)
    owners, slot_rank = slot_places(owner_of)
    slot_grad = jnp.zeros((N_OWNER, CAPACITY, BLOCK, BLOCK), jnp.bfloat16).at[owners, slot_rank].set(grad_sum.astype(jnp.bfloat16))
    results = lax.map(one_slot, (flatten_slots(slot_grad), flatten_slots(stats_left), flatten_slots(stats_right), flatten_slots(basis_left), flatten_slots(basis_right), flatten_slots(moment_first), flatten_slots(moment_second)))
    left_new, right_new, first_new, second_new, slot_update = [item.reshape((N_OWNER, CAPACITY) + item.shape[1:]) for item in results]
    update = slot_update[owners, slot_rank]
    return (left_new, right_new, first_new, second_new, update)
```

```python
import jax
import jax.numpy as jnp
from jax import lax
from jax.experimental import pallas as pl
from jax.experimental.pallas import tpu as pltpu
from jax.sharding import PartitionSpec as P

BETA_FIRST = 0.9
BETA_SECOND = 0.95
EPSILON = 1e-08
MESH = pl.DeviceIdType.MESH
BF = jnp.bfloat16
F32 = jnp.float32
NY, NX, NZ = 8, 4, 16
NB, PADB = 144, 256
SLOTS = 5
SUBS, SUBROWS = 3, 48
PAIRS = ((0, 1), (2, 3), (4, 4))
PAIR_CORE = (0, 1, 0)


def mm(a, b):
    return jnp.dot(a, b, preferred_element_type=F32)


def mm_t(a, b):
    return lax.dot_general(a, b, (((1,), (1,)), ((), ())), preferred_element_type=F32)


def iota(shape, axis):
    return lax.broadcasted_iota(jnp.int32, shape, axis)


def onehot(a, b):
    return jnp.where(a == b, 1.0, 0.0).astype(BF)


def kernel(
    grad, own_col, own_row, stats_l, stats_r, basis_l, basis_r, mom1, mom2,
    out_l, out_r, out_1, out_2, out_u,
    go, gx, chunk, rs_recv, rs_send, summed, place, v1, w1, xs1, gall,
    ql, qr, qrs, sl, sr, m1, m2, arot, pm, perm2, perm3, ohfin, pick,
    bmsg, bb, ub, w2, xs2, yb,
    s_in, s_core, r_core, s_rs, r_rs, s_cag, r_cag, s_z1, r_z1, s_x1, r_x1,
    s_ag, r_ag, s_sib, r_sib, s_b, r_b, s_z2, r_z2, s_x2, r_x2, s_y, r_y,
):
    rep = lax.axis_index("replica")
    own = lax.axis_index("owner")
    y, c = rep // 2, rep % 2
    z, x = own // NX, own % NX
    sib = (y * 2 + (1 - c), own)
    zhalf = z // 8
    active = c == zhalf

    def at_y(yy, cc):
        return (lax.rem(yy + 2 * NY, NY) * 2 + cc, own)

    def at_z(zz):
        return (rep, zz * NX + x)

    def at_x(xx):
        return (rep, z * NX + xx)

    def remote(src, dst, ssem, rsem, dev):
        return pltpu.make_async_remote_copy(
            src_ref=src, dst_ref=dst, send_sem=ssem, recv_sem=rsem, device_id=dev, device_id_type=MESH
        )

    half = pl.ds(pl.multiple_of(c * 256, 256), 256)
    other = pl.ds(pl.multiple_of((1 - c) * 256, 256), 256)
    loads = [pltpu.make_async_copy(grad.at[:, half], go, s_in.at[0])]
    loads += [
        pltpu.make_async_copy(src, dst, s_in.at[1 + i])
        for i, (src, dst) in enumerate(
            ((basis_l, ql), (basis_r, qr), (stats_l, sl), (stats_r, sr), (mom1, m1), (mom2, m2))
        )
    ]
    swaps = []
    for i, k in enumerate((1, 3, 4)):
        for h in range(2):
            swaps.append(
                pltpu.make_async_copy(
                    basis_r.at[k, :, h], qrs.at[i, :, 1 - h], s_in.at[7 + 2 * i + h]
                )
            )
    loads[0].start()

    barrier = pltpu.get_barrier_semaphore()
    for d in range(1, 16):
        pl.semaphore_signal(barrier, inc=1, device_id=(lax.rem(rep + d, 16), own), device_id_type=MESH)
    for d in range(1, NZ):
        pl.semaphore_signal(barrier, inc=1, device_id=at_z(lax.rem(z + d, NZ)), device_id_type=MESH)
    for d in range(1, NX):
        pl.semaphore_signal(barrier, inc=1, device_id=at_x(lax.rem(x + d, NX)), device_id_type=MESH)
    pl.semaphore_wait(barrier, 15 + NZ - 1 + NX - 1)

    def core_copy(j):
        rows = pl.ds(j * 384, 384)
        return remote(grad.at[rows, other], gx.at[rows], s_core.at[j], r_core.at[j], sib)

    for j in range(3):
        core_copy(j).start()
    for d in loads[1:] + swaps:
        d.start()
    out_of = iota((128, 1), 0)
    perm1 = onehot(iota((128, 128), 1), (out_of % 16) * 8 + out_of // 16)
    loads[0].wait()
    for j in range(3):
        core_copy(j).wait_recv()
        for g in range(3 * j, 3 * j + 3):
            rows = pl.ds(g * 128, 128)
            both = (mm(perm1, go[rows, :]) + mm(perm1, gx[rows, :])).astype(BF)
            for t in range(NY):
                chunk[t, pl.ds(g * 16, 16), :] = both[t * 16 : t * 16 + 16]

    def rs_copy(d, s, j):
        rows = pl.ds(j * SUBROWS, SUBROWS)
        sign = 1 - 2 * d
        if s == 0:
            lanes = pl.ds(d * 128, 128)
            src = chunk.at[lax.rem(y + 4, NY), rows, lanes]
            dst = rs_recv.at[d, s, rows, lanes]
        else:
            src = rs_send.at[d, s - 1, rows]
            dst = rs_recv.at[d, s, rows]
        return remote(src, dst, s_rs.at[d, s, j], r_rs.at[d, s, j], at_y(y + sign, c))

    def rs_step(s):
        for j in range(SUBS):
            for d in range(2):
                rows = pl.ds(j * SUBROWS, SUBROWS)
                t = lax.rem(y + (1 - 2 * d) * (4 - s) + NY, NY)
                rs_copy(d, s - 1, j).wait_recv()
                if s == 1:
                    lanes = pl.ds(d * 128, 128)
                    rest = pl.ds((1 - d) * 128, 128)
                    rs_send[d, 0, rows, lanes] = (
                        chunk[t, rows, lanes].astype(F32) + rs_recv[d, 0, rows, lanes].astype(F32)
                    ).astype(BF)
                    rs_send[d, 0, rows, rest] = chunk[t, rows, rest]
                else:
                    rs_send[d, s - 1, rows] = (
                        chunk[t, rows].astype(F32) + rs_recv[d, s - 1, rows].astype(F32)
                    ).astype(BF)
                rs_copy(d, s, j).start()

    for j in range(SUBS):
        for d in range(2):
            rs_copy(d, 0, j).start()

    o_row = own_row[...]
    e_row = onehot(iota((128, PADB), 0), o_row)
    before = mm(e_row, onehot_lt(iota((PADB, PADB), 0), iota((PADB, PADB), 1)))
    k_row = jnp.sum(before * e_row.astype(F32), axis=0, keepdims=True).astype(jnp.int32)
    zr, xr = o_row >> 2, o_row & 3
    code = jnp.where((zr >> 3) == c, (k_row * 8 + (zr & 7)) * 16 + xr, -64)
    for q in range(4):
        place[q] = onehot(iota((640, PADB), 0), code + 4 * q)
    summed[:, pl.ds(NB, PADB - NB), :] = jnp.zeros((2, PADB - NB, 256), BF)
    rs_step(1)

    o_col = own_col[...]
    e_col = onehot(iota((PADB, 128), 1), o_col)
    before = mm(onehot_lt(iota((PADB, PADB), 1), iota((PADB, PADB), 0)), e_col)
    k_col = jnp.sum(before * e_col.astype(F32), axis=1, keepdims=True).astype(jnp.int32)
    zc, xc = o_col >> 2, o_col & 3
    ohfin[...] = onehot(iota((NB, 256), 1), ((k_col >> 1) * 64 + xc * 16 + zc)[:NB])
    upper = ((k_col + y) & 1)[:NB]
    rho = iota((1, 512), 1)
    natural = ((rho & 15) * 4 + ((rho >> 4) & 3)) * 8 + (rho >> 6)
    pm[...] = onehot(iota((512, 512), 0), natural)
    rs_step(2)

    for d in loads[1:] + swaps:
        d.wait()
    mine = onehot(iota((32, 512), 1), iota((32, 512), 0) + rep * 32)
    for k in range(SLOTS):
        arot[k] = mm(mm_t(mine, ql[k]).astype(BF), pm[...]).astype(BF)
    rs_step(3)

    j2 = iota((256, 1), 0)
    perm2[...] = onehot(iota((256, 256), 1), (j2 & 15) * 16 + ((j2 >> 4) & 3) * 4 + (j2 >> 6))
    j3 = iota((512, 1), 0)
    perm3[...] = onehot(
        iota((512, 512), 1), (j3 & 15) * 32 + (j3 >> 7) * 8 + ((j3 >> 4) & 7)
    )
    for j in range(SUBS):
        rows = pl.ds(j * SUBROWS, SUBROWS)
        for d in range(2):
            rs_copy(d, 3, j).wait_recv()
        summed[c, rows] = (
            chunk[y, rows].astype(F32) + rs_recv[0, 3, rows].astype(F32) + rs_recv[1, 3, rows].astype(F32)
        ).astype(BF)
    to_sib = remote(
        summed.at[c, pl.ds(0, NB)], summed.at[c, pl.ds(0, NB)], s_cag.at[0], r_cag.at[0], sib
    )
    to_sib.start()
    from_sib = remote(
        summed.at[1 - c, pl.ds(0, NB)], summed.at[1 - c, pl.ds(0, NB)], s_cag.at[0], r_cag.at[0], sib
    )
    from_sib.wait_recv()

    placed = mm(place[0], summed[0, :, pl.ds(0, 128)])
    placed += mm(place[1], summed[0, :, pl.ds(128, 128)])
    placed += mm(place[2], summed[1, :, pl.ds(0, 128)])
    placed += mm(place[3], summed[1, :, pl.ds(128, 128)])
    v1[...] = placed.astype(BF).reshape(SLOTS, 8, 16, 128)

    def z1_copy(j):
        low = lax.rem(z + j, 8)
        return remote(v1.at[:, low], w1.at[:, z], s_z1.at[j], r_z1.at[z], at_z(c * 8 + low))

    for j in range(1, 8):
        z1_copy(j).start()

    @pl.when(jnp.logical_not(active))
    def _():
        z1_copy(0).start()

    @pl.when(active)
    def _():
        w1[:, z] = v1[:, lax.rem(z, 8)]

    def ag_copy(d, s, k):
        sign = 1 - 2 * d
        origin = lax.rem(y - sign * s + NY, NY)
        rows = pl.ds(pl.multiple_of(origin * 64, 64), 64)
        ref = gall.at[k, rows] if s < 3 else gall.at[k, rows, pl.ds(d * 256, 256)]
        return remote(ref, ref, s_ag.at[d, s, k], r_ag.at[d, s, k], at_y(y + sign, c))

    def ag_arrival(d, s, k):
        sign = 1 - 2 * d
        origin = lax.rem(y - sign * (s + 1) + NY, NY)
        rows = pl.ds(pl.multiple_of(origin * 64, 64), 64)
        return gall.at[k, rows] if s < 3 else gall.at[k, rows, pl.ds(d * 256, 256)]

    def ag_wait(d, s, k):
        ref = ag_arrival(d, s, k)
        remote(ref, ref, s_ag.at[d, s, k], r_ag.at[d, s, k], at_y(y, c)).wait_recv()

    def sib_copy(i, k):
        if i == 8:
            ref = gall.at[k, pl.ds(pl.multiple_of(y * 64, 64), 64)]
        else:
            ref = ag_arrival(i // 4, i % 4, k)
        return remote(ref, ref, s_sib.at[i, k], r_sib.at[i, k], sib)

    def x1_copy(j):
        to = lax.rem(x + j, NX)
        rows = pl.ds(pl.multiple_of(y * 64 + x * 16, 16), 16)
        return remote(xs1.at[:, to], gall.at[:, rows], s_x1.at[j - 1], r_x1.at[x], at_x(to))

    def x1_wait(j):
        src = lax.rem(x + j, NX)
        rows = pl.ds(pl.multiple_of(y * 64 + src * 16, 16), 16)
        remote(xs1.at[:, src], gall.at[:, rows], s_x1.at[0], r_x1.at[src], at_x(src)).wait_recv()

    @pl.when(active)
    def _():
        for j in range(1, NZ):
            src = lax.rem(z + j, NZ)
            remote(v1.at[:, 0], w1.at[:, src], s_z1.at[0], r_z1.at[src], at_z(src)).wait_recv()
        for k in range(SLOTS):
            regrouped = mm(perm2[...], w1[k].reshape(256, 128)).astype(BF)
            for to in range(NX):
                for q in range(4):
                    n = (to * 4 + q) * 16
                    xs1[k, to, :, pl.ds(q * 128, 128)] = regrouped[n : n + 16]
        for j in range(1, NX):
            x1_copy(j).start()
        for k in range(SLOTS):
            gall[k, pl.ds(pl.multiple_of(y * 64 + x * 16, 16), 16), :] = xs1[k, x]
        for j in range(1, NX):
            x1_wait(j)

    lane_low = iota((32, 128), 1) < 64
    back = {}

    def slot_products(k):
        h = mm(arot[k], gall[k]).astype(BF)
        rotated = mm(h, qr[k].reshape(512, 512))
        first = BETA_FIRST * m1[k] + (1.0 - BETA_FIRST) * rotated
        second = BETA_SECOND * m2[k] + (1.0 - BETA_SECOND) * rotated * rotated
        out_1[k] = first
        out_2[k] = second
        direction = (first / (jnp.sqrt(second) + EPSILON)).astype(BF)
        if k in (0, 2, 4):
            back[k, 0] = mm_t(direction, qr[k].reshape(512, 512)).astype(BF)
        if k in (1, 3, 4):
            back[k, 1] = mm_t(direction, qrs[(k - 1) // 2 if k < 4 else 2].reshape(512, 512)).astype(BF)

    def b_copy(p, yy):
        return remote(bmsg.at[p, yy], bb.at[p, rep], s_b.at[p, yy], r_b.at[p, rep], (yy * 2 + PAIR_CORE[p], own))

    def send_back(p):
        a, b = PAIRS[p]
        for yy in range(NY):
            lanes = slice((yy // 2) * 128, (yy // 2) * 128 + 128)
            lo, hi = back[a, 0][:, lanes], back[b, 1][:, lanes]
            bmsg[p, yy] = jnp.where(lane_low, lo, hi) if yy % 2 == 0 else jnp.where(lane_low, hi, lo)
        for yy in range(NY):
            here = jnp.logical_and(yy == y, c == PAIR_CORE[p])

            @pl.when(jnp.logical_not(here))
            def _():
                b_copy(p, yy).start()

            @pl.when(here)
            def _():
                bb[p, rep] = bmsg[p, yy]

    def stat_products(k):
        columns = mm_t(mine, gall[k]).astype(BF)
        right = mm(columns, gall[k])
        out_r[k] = (BETA_SECOND * sr[k].astype(F32) + (1.0 - BETA_SECOND) * right).astype(BF)
        rows = mm(pm[pl.ds(pl.multiple_of(rep * 32, 32), 32), :], gall[k]).astype(BF)
        left = mm_t(rows, gall[k])
        high = left.astype(BF)
        low = (left - high.astype(F32)).astype(BF)
        left = mm_t(high, pm[...]) + mm_t(low, pm[...])
        out_l[k] = (BETA_SECOND * sl[k].astype(F32) + (1.0 - BETA_SECOND) * left).astype(BF)

    for w in range(SLOTS + 4):

        @pl.when(active)
        def _():
            for s in range(4, -1, -1):
                k = w - s
                if k < 0 or k >= SLOTS:
                    continue
                for d in range(2):
                    if s > 0:
                        ag_wait(d, s - 1, k)
                    if s < 4:
                        ag_copy(d, s, k).start()
                    if s > 0:
                        sib_copy(d * 4 + s - 1, k).start()
                if s == 0:
                    sib_copy(8, k).start()

        if w >= 4:
            k = w - 4

            @pl.when(jnp.logical_not(active))
            def _():
                for i in range(8):
                    ref = ag_arrival(i // 4, i % 4, k)
                    remote(ref, ref, s_sib.at[i, k], r_sib.at[i, k], sib).wait_recv()
                sib_copy(8, k).wait_recv()

            slot_products(k)
            if k in (1, 3, 4):
                send_back((1, 3, 4).index(k))

    for i in range(8):
        j = iota((256, 256), 1)
        l = iota((256, 256), 0)
        wanted = (l & 64) == ((l >> 7) << 6)
        pick[i] = jnp.where(
            ((l & 63) == (j & 31) + 32 * c) & wanted & ((j >> 5) == i), 1.0, 0.0
        ).astype(BF)
    yb[pl.ds(3, 1)] = jnp.zeros((1, NX, 8, 16, 128), BF)

    def z2_copy(p, j):
        to = lax.rem(z + j, NZ)
        return remote(
            ub.at[p, pl.ds(pl.multiple_of(to * 32, 32), 32)], w2.at[p, z], s_z2.at[p, j - 1], r_z2.at[p, z], at_z(to)
        )

    def x2_copy(p, j):
        to = lax.rem(x + j, NX)
        return remote(xs2.at[p, to], yb.at[p, x], s_x2.at[p, j - 1], r_x2.at[p, x], at_x(to))

    def y_copy(p):
        return remote(yb.at[p], yb.at[p], s_y.at[p], r_y.at[p], sib)

    def update_products(p):
        for d in range(1, 16):
            src = lax.rem(rep + d, 16)
            remote(bmsg.at[p, 0], bb.at[p, src], s_b.at[p, 0], r_b.at[p, src], (src, own)).wait_recv()
        a, b = PAIRS[p]
        columns = bb[p].reshape(512, 128)
        if a == b:
            ub[p] = mm(ql[a], columns).astype(BF)
        else:
            swap = jnp.where(iota((512, 128), 1) < 64, 0, 1) == (y & 1)
            ub[p] = jnp.where(swap, mm(ql[a], columns), mm(ql[b], columns)).astype(BF)
        for j in range(1, NZ):
            z2_copy(p, j).start()
        w2[p, z] = ub[p, pl.ds(pl.multiple_of(z * 32, 32), 32)]

    def update_regroup(p):
        for j in range(1, NZ):
            src = lax.rem(z + j, NZ)
            remote(ub.at[p, pl.ds(0, 32)], w2.at[p, src], s_z2.at[p, 0], r_z2.at[p, src], at_z(src)).wait_recv()
        xs2[p] = mm(perm3[...], w2[p].reshape(512, 128)).astype(BF).reshape(NX, 8, 16, 128)
        for j in range(1, NX):
            x2_copy(p, j).start()
        yb[p, x] = xs2[p, x]

    def update_share(p):
        for j in range(1, NX):
            src = lax.rem(x + j, NX)
            remote(xs2.at[p, 0], yb.at[p, src], s_x2.at[p, 0], r_x2.at[p, src], at_x(src)).wait_recv()
        y_copy(p).start()

    for core in range(2):
        mine_of = [p for p in range(3) if PAIR_CORE[p] == core]

        @pl.when(c == core)
        def _():
            for p in mine_of:
                update_products(p)
            for k in range(SLOTS):
                stat_products(k)
            for p in mine_of:
                update_regroup(p)
            for p in mine_of:
                update_share(p)
            for p in range(3):
                if PAIR_CORE[p] != core:
                    y_copy(p).wait_recv()

    upper_f = upper.astype(F32)
    total = jnp.zeros((NB, 256), F32)
    for i in range(8):
        rows = yb[:, :, i].reshape(256, 128)
        found = mm(ohfin[...], rows)
        both = jnp.concatenate([found * (1.0 - upper_f), found * upper_f], axis=1).astype(BF)
        total += mm(both, pick[i])
    out_u[...] = total.astype(BF)

    for j in range(3):
        core_copy(j).wait_send()
    for s in range(4):
        for j in range(SUBS):
            for d in range(2):
                rs_copy(d, s, j).wait_send()
    to_sib.wait_send()
    for j in range(1, 8):
        z1_copy(j).wait_send()

    @pl.when(jnp.logical_not(active))
    def _():
        z1_copy(0).wait_send()

    @pl.when(active)
    def _():
        for j in range(1, NX):
            x1_copy(j).wait_send()
        for k in range(SLOTS):
            for s in range(4):
                for d in range(2):
                    ag_copy(d, s, k).wait_send()
                    sib_copy(d * 4 + s, k).wait_send()
            sib_copy(8, k).wait_send()

    for p in range(3):
        for yy in range(NY):

            @pl.when(jnp.logical_not(jnp.logical_and(yy == y, c == PAIR_CORE[p])))
            def _():
                b_copy(p, yy).wait_send()

        @pl.when(c == PAIR_CORE[p])
        def _():
            for j in range(1, NZ):
                z2_copy(p, j).wait_send()
            for j in range(1, NX):
                x2_copy(p, j).wait_send()
            y_copy(p).wait_send()


def onehot_lt(a, b):
    return jnp.where(a < b, 1.0, 0.0).astype(BF)


def shards(grad_parts, owner_of, stats_left, stats_right, basis_left, basis_right, moment_first, moment_second):
    blocks = owner_of.shape[0]
    padded = jnp.pad(owner_of[:, 0], (0, PADB - blocks), constant_values=-1)
    anywhere = pl.BlockSpec(memory_space=pl.ANY)
    vmem = pl.BlockSpec(memory_space=pltpu.VMEM)
    rows = (SLOTS, 32, 512)
    dma = pltpu.SemaphoreType.DMA
    scratch = [
        pltpu.VMEM((1152, 256), BF),
        pltpu.VMEM((1152, 256), BF),
        pltpu.VMEM((NY, NB, 256), BF),
        pltpu.VMEM((2, 4, NB, 256), BF),
        pltpu.VMEM((2, 3, NB, 256), BF),
        pltpu.VMEM((2, PADB, 256), BF),
        pltpu.VMEM((4, 640, PADB), BF),
        pltpu.VMEM((SLOTS, 8, 16, 128), BF),
        pltpu.VMEM((SLOTS, NZ, 16, 128), BF),
        pltpu.VMEM((SLOTS, NX, 16, 512), BF),
        pltpu.VMEM((SLOTS, 512, 512), BF),
        pltpu.VMEM((SLOTS, 512, 512), BF),
        pltpu.VMEM((SLOTS, 4, 2, 64, 512), BF),
        pltpu.VMEM((3, 4, 2, 64, 512), BF),
        pltpu.VMEM(rows, BF),
        pltpu.VMEM(rows, BF),
        pltpu.VMEM(rows, F32),
        pltpu.VMEM(rows, F32),
        pltpu.VMEM(rows, BF),
        pltpu.VMEM((512, 512), BF),
        pltpu.VMEM((256, 256), BF),
        pltpu.VMEM((512, 512), BF),
        pltpu.VMEM((NB, 256), BF),
        pltpu.VMEM((8, 256, 256), BF),
        pltpu.VMEM((3, NY, 32, 128), BF),
        pltpu.VMEM((3, 16, 32, 128), BF),
        pltpu.VMEM((3, 512, 128), BF),
        pltpu.VMEM((3, NZ, 32, 128), BF),
        pltpu.VMEM((3, NX, 8, 16, 128), BF),
        pltpu.VMEM((4, NX, 8, 16, 128), BF),
        dma((13,)),
        dma((3,)), dma((3,)),
        dma((2, 4, SUBS)), dma((2, 4, SUBS)),
        dma((1,)), dma((1,)),
        dma((8,)), dma((NZ,)),
        dma((3,)), dma((NX,)),
        dma((2, 4, SLOTS)), dma((2, 4, SLOTS)),
        dma((9, SLOTS)), dma((9, SLOTS)),
        dma((3, NY)), dma((3, 16)),
        dma((3, NZ - 1)), dma((3, NZ)),
        dma((3, NX - 1)), dma((3, NX)),
        dma((3,)), dma((3,)),
    ]
    new_left, new_right, new_first, new_second, picked = pl.pallas_call(
        kernel,
        out_shape=(
            jax.ShapeDtypeStruct(rows, BF),
            jax.ShapeDtypeStruct(rows, BF),
            jax.ShapeDtypeStruct(rows, F32),
            jax.ShapeDtypeStruct(rows, F32),
            jax.ShapeDtypeStruct((blocks, 256), BF),
        ),
        in_specs=[anywhere, vmem, vmem] + [anywhere] * 6,
        out_specs=(vmem,) * 5,
        scratch_shapes=scratch,
        compiler_params=pltpu.CompilerParams(
            collective_id=0, has_side_effects=True, vmem_limit_bytes=56 * 1024 * 1024
        ),
    )(
        grad_parts[0].reshape(blocks * 8, 512),
        padded[:, None],
        padded[None, :],
        stats_left[0],
        stats_right[0],
        basis_left[0],
        basis_right[0].reshape(SLOTS, 4, 2, 64, 512),
        moment_first[0],
        moment_second[0],
    )
    update = picked.reshape(blocks, 8, 32)
    return (new_left[None], new_right[None], new_first[None], new_second[None], update)


def solution(mesh):
    return jax.shard_map(
        shards,
        mesh=mesh,
        in_specs=(
            P("replica", None, "owner", None),
            P(),
            P("owner", None, "replica", None),
            P("owner", None, "replica", None),
            P("owner", None, None, None),
            P("owner", None, None, None),
            P("owner", None, "replica", None),
            P("owner", None, "replica", None),
        ),
        out_specs=(
            P("owner", None, "replica", None),
            P("owner", None, "replica", None),
            P("owner", None, "replica", None),
            P("owner", None, "replica", None),
            P(None, "owner", "replica"),
        ),
        check_vma=False,
    )
```

```python
import jax
import jax.numpy as jnp
from jax import lax
from jax.experimental import pallas as pl
from jax.experimental.pallas import tpu as pltpu
from jax.sharding import PartitionSpec as P

BETA_FIRST = 0.9
BETA_SECOND = 0.95
EPSILON = 1e-08
MESH = pl.DeviceIdType.MESH
BF = jnp.bfloat16
F32 = jnp.float32
NY, NX, NZ = 8, 4, 16
NB, PADB = 144, 256
SLOTS = 5
SUBS, SUBROWS = 3, 48
PAIRS = ((0, 1), (2, 3), (4, 4))
PAIR_CORE = (0, 1, 0)


def mm(a, b):
    return jnp.dot(a, b, preferred_element_type=F32)


def mm_t(a, b):
    return lax.dot_general(a, b, (((1,), (1,)), ((), ())), preferred_element_type=F32)


def iota(shape, axis):
    return lax.broadcasted_iota(jnp.int32, shape, axis)


def onehot(a, b):
    return jnp.where(a == b, 1.0, 0.0).astype(BF)


def kernel(
    grad, own_row, stats_l, stats_r, basis_l, basis_r, mom1, mom2,
    out_l, out_r, out_1, out_2, out_u,
    go, gx, chunk, rs_recv, rs_send, summed, place, v1, w1, xs1, gall,
    ql, qr, qrs, sl, sr, m1, m2, ol, orr, o1, o2, qlt, hsend, hrecv, gf, pm, perm2, perm3, perm4, oh2, wbuf,
    bmsg, bb, ub, ub4, w2, w24, xs2, yb,
    s_in, s_out, s_core, r_core, s_rs, r_rs, s_cag, r_cag, s_z1, r_z1, s_x1, r_x1,
    s_h, r_h, s_own, r_own, s_ag, r_ag, s_sib, r_sib, s_b, r_b, s_z2, r_z2, s_x2, r_x2, s_y, r_y,
):
    rep = lax.axis_index("replica")
    own = lax.axis_index("owner")
    y, c = rep // 2, rep % 2
    z, x = own // NX, own % NX
    sib = (y * 2 + (1 - c), own)
    zhalf = z // 8
    active = c == zhalf

    def at_y(yy, cc):
        return (lax.rem(yy + 2 * NY, NY) * 2 + cc, own)

    def at_z(zz):
        return (rep, zz * NX + x)

    def at_x(xx):
        return (rep, z * NX + xx)

    def remote(src, dst, ssem, rsem, dev):
        return pltpu.make_async_remote_copy(
            src_ref=src, dst_ref=dst, send_sem=ssem, recv_sem=rsem, device_id=dev, device_id_type=MESH
        )

    half = pl.ds(pl.multiple_of(c * 256, 256), 256)
    other = pl.ds(pl.multiple_of((1 - c) * 256, 256), 256)
    loads = [pltpu.make_async_copy(grad.at[:, half], go, s_in.at[0])]
    loads += [
        pltpu.make_async_copy(src, dst, s_in.at[1 + i])
        for i, (src, dst) in enumerate(
            ((basis_l, ql), (basis_r, qr), (stats_l, sl), (stats_r, sr), (mom1, m1), (mom2, m2))
        )
    ]
    swaps = []
    for i, k in enumerate((1, 3, 4)):
        for h in range(2):
            swaps.append(
                pltpu.make_async_copy(
                    basis_r.at[k, :, h], qrs.at[i, :, 1 - h], s_in.at[7 + 2 * i + h]
                )
            )
    loads[0].start()
    drains = []

    barrier = pltpu.get_barrier_semaphore()
    for d in range(1, 16):
        pl.semaphore_signal(barrier, inc=1, device_id=(lax.rem(rep + d, 16), own), device_id_type=MESH)
    for d in range(1, NZ):
        pl.semaphore_signal(barrier, inc=1, device_id=at_z(lax.rem(z + d, NZ)), device_id_type=MESH)
    for d in range(1, NX):
        pl.semaphore_signal(barrier, inc=1, device_id=at_x(lax.rem(x + d, NX)), device_id_type=MESH)
    pl.semaphore_wait(barrier, 15 + NZ - 1 + NX - 1)

    def core_copy(j):
        rows = pl.ds(j * 384, 384)
        return remote(grad.at[rows, other], gx.at[rows], s_core.at[j], r_core.at[j], sib)

    def rs_target(d, s):
        t = lax.rem(y + (1 - 2 * d) * (4 - s) + NY, NY)
        return (t // 4) * 2 + t % 2, c == (t % 4) // 2

    def rs_copy(d, s, j):
        rows = pl.ds(j * SUBROWS, SUBROWS)
        if s == 0:
            lanes = pl.ds(d * 256, 256)
            src = chunk.at[rs_target(d, 0)[0], rows, lanes]
            dst = rs_recv.at[d, s, rows, lanes]
        else:
            src = rs_send.at[d, s - 1, rows]
            dst = rs_recv.at[d, s, rows]
        return remote(src, dst, s_rs.at[d, s, j], r_rs.at[d, s, j], at_y(y + 1 - 2 * d, c))

    for j in range(3):
        core_copy(j).start()
    for d in loads[1:] + swaps:
        d.start()

    out_of = iota((128, 1), 0)
    perm1 = onehot(iota((128, 128), 1), (out_of % 16) * 8 + out_of // 16)
    o_row = own_row[...]
    e_row = onehot(iota((128, PADB), 0), o_row)
    before = mm(e_row, onehot_lt(iota((PADB, PADB), 0), iota((PADB, PADB), 1)))
    k_row = jnp.sum(before * e_row.astype(F32), axis=0, keepdims=True).astype(jnp.int32)
    zr, xr = o_row >> 2, o_row & 3
    code = jnp.where((zr >> 3) == c, (k_row * 8 + (zr & 7)) * 16 + xr, -64)
    for q in range(4):
        place[q] = onehot(iota((640, PADB), 0), code + 4 * q)
    side = jnp.where(k_row == 4, x >> 1, (k_row + y) & 1)
    slot_code = side * 256 + (k_row >> 1) * 64 + xr * 16 + zr
    summed[pl.ds(NB, PADB - NB), :] = jnp.zeros((PADB - NB, 512), BF)

    loads[0].wait()
    for j in range(3):
        core_copy(j).wait_recv()
        for g in range(3 * j, 3 * j + 3):
            rows = pl.ds(g * 128, 128)
            both = (mm(perm1, go[rows, :]) + mm(perm1, gx[rows, :])).astype(BF)
            for i in range(8):
                for q in range(2):
                    chunk[(i // 4) * 2 + q, pl.ds(g * 16, 16), pl.ds((i % 4) * 128, 128)] = both[
                        i * 16 : i * 16 + 16, q * 128 : q * 128 + 128
                    ]

        @pl.when(rs_target(0, 0)[1])
        def _():
            for d in range(2):
                rs_copy(d, 0, j).start()

    drains.append(lambda: [core_copy(j).wait_send() for j in range(3)])

    for d in loads[1:] + swaps:
        d.wait()
    r_col = iota((256, 1), 0)
    held = ((r_col & 15) * 4 + ((r_col >> 4) & 3)) * 8 + (y // 4) * 4 + (r_col >> 6)
    held_rows = onehot(iota((256, 512), 1), held)
    same = onehot(iota((512, 512), 0), iota((512, 512), 1))

    def turn_basis(k):
        qlt[k] = mm_t(same, mm(held_rows, ql[k]).astype(BF)).astype(BF)

    turn_basis(0)

    for s in range(1, 4):
        for j in range(SUBS):
            for d in range(2):
                rows = pl.ds(j * SUBROWS, SUBROWS)
                t, here = rs_target(d, s)

                @pl.when(here)
                def _():
                    rs_copy(d, s - 1, j).wait_recv()
                    if s == 1:
                        lanes = pl.ds(d * 256, 256)
                        rest = pl.ds((1 - d) * 256, 256)
                        rs_send[d, 0, rows, lanes] = (
                            chunk[t, rows, lanes].astype(F32) + rs_recv[d, 0, rows, lanes].astype(F32)
                        ).astype(BF)
                        rs_send[d, 0, rows, rest] = chunk[t, rows, rest]
                    else:
                        rs_send[d, s - 1, rows] = (
                            chunk[t, rows].astype(F32) + rs_recv[d, s - 1, rows].astype(F32)
                        ).astype(BF)
                    rs_copy(d, s, j).start()

        if s == 1:
            turn_basis(1)
            turn_basis(2)
        if s == 2:
            turn_basis(3)
            turn_basis(4)
        if s == 3:
            j2 = iota((256, 1), 0)
            perm2[...] = onehot(iota((256, 256), 1), (j2 & 15) * 16 + ((j2 >> 4) & 3) * 4 + (j2 >> 6))
            rho = iota((1, 512), 1)
            natural = ((rho & 15) * 4 + ((rho >> 4) & 3)) * 8 + (rho >> 8) * 4 + ((rho >> 6) & 3)
            pm[...] = onehot(iota((512, 512), 0), natural)

    def share_sum(j):
        ref = summed.at[pl.ds(j * SUBROWS, SUBROWS)]
        return remote(ref, ref, s_cag.at[j], r_cag.at[j], sib)

    last, sums_here = rs_target(0, 4)

    @pl.when(sums_here)
    def _():
        for j in range(SUBS):
            rows = pl.ds(j * SUBROWS, SUBROWS)
            for d in range(2):
                rs_copy(d, 3, j).wait_recv()
            summed[rows] = (
                chunk[last, rows].astype(F32) + rs_recv[0, 3, rows].astype(F32) + rs_recv[1, 3, rows].astype(F32)
            ).astype(BF)
            share_sum(j).start()

    @pl.when(jnp.logical_not(sums_here))
    def _():
        for j in range(SUBS):
            share_sum(j).wait_recv()

    def drain_2():
        for s in range(4):
            for d in range(2):

                @pl.when(rs_target(d, s)[1])
                def _():
                    for j in range(SUBS):
                        rs_copy(d, s, j).wait_send()

        @pl.when(sums_here)
        def _():
            for j in range(SUBS):
                share_sum(j).wait_send()

    drains.append(drain_2)

    def z1_copy(k, j):
        low = lax.rem(z + j + 4 * active.astype(jnp.int32), 8)
        return remote(v1.at[k, low], w1.at[k, z], s_z1.at[k, j], r_z1.at[k, z], at_z(c * 8 + low))

    def fill_slots(k, n):
        rows = pl.ds(k * 128, n * 128)
        placed = mm(place[0, rows], summed[:, pl.ds(0, 128)])
        for q in range(1, 4):
            placed += mm(place[q, rows], summed[:, pl.ds(q * 128, 128)])
        v1[pl.ds(k, n)] = placed.astype(BF).reshape(n, 8, 16, 128)
        for kk in range(k, k + n):
            for j in (0, 1, 7, 2, 6, 3, 5):
                z1_copy(kk, j).start()

            @pl.when(jnp.logical_not(active))
            def _():
                z1_copy(kk, 4).start()

        @pl.when(active)
        def _():
            w1[pl.ds(k, n), z] = v1[pl.ds(k, n), lax.rem(z, 8)]

    fill_slots(0, 1)
    fill_slots(1, 4)

    def drain_3():
        for k in range(SLOTS):
            for j in (0, 1, 7, 2, 6, 3, 5):
                z1_copy(k, j).wait_send()

        @pl.when(jnp.logical_not(active))
        def _():
            for k in range(SLOTS):
                z1_copy(k, 4).wait_send()

        @pl.when(active)
        def _():
            for k in range(SLOTS):
                for j in range(1, NX):
                    x1_copy(k, j).wait_send()

    drains.append(drain_3)

    mine = onehot(iota((32, 512), 1), iota((32, 512), 0) + rep * 32)

    def x1_copy(k, j):
        to = lax.rem(x + j, NX)
        rows = pl.ds(pl.multiple_of(x * 16, 16), 16)
        return remote(xs1.at[k, to], gall.at[k, y, :, rows], s_x1.at[k, j - 1], r_x1.at[k, x], at_x(to))

    def x1_wait(k, j):
        src = lax.rem(x + j, NX)
        rows = pl.ds(pl.multiple_of(src * 16, 16), 16)
        remote(xs1.at[k, src], gall.at[k, y, :, rows], s_x1.at[k, 0], r_x1.at[k, src], at_x(src)).wait_recv()

    def regroup_slot(k):
        for j in range(1, NZ):
            src = lax.rem(z + j, NZ)
            remote(v1.at[k, 0], w1.at[k, src], s_z1.at[k, 0], r_z1.at[k, src], at_z(src)).wait_recv()
        xs1[k] = mm(perm2[...], w1[k].reshape(256, 128)).astype(BF).reshape(NX, 4, 16, 128)
        for j in (2, 1, 3):
            x1_copy(k, j).start()
        gall[k, y, :, pl.ds(pl.multiple_of(x * 16, 16), 16)] = xs1[k, x]

    def h_copy(k, dy, cc):
        to = lax.rem(y + dy, NY) * 2 + cc
        return remote(hsend.at[k, to], hrecv.at[k, y], s_h.at[k, dy, cc], r_h.at[k, y], (to, own))

    def h_wait(k, dy):
        t = lax.rem(y + dy, NY)
        remote(hsend.at[k, 0], hrecv.at[k, t], s_h.at[k, 0, 0], r_h.at[k, t], sib).wait_recv()

    def own_copy(k):
        ref = gall.at[k, y]
        return remote(ref, ref, s_own.at[k], r_own.at[k], sib)

    far_first = (4, 3, 5, 2, 6, 1, 7)

    def left_product(k):
        for j in range(1, NX):
            x1_wait(k, j)
        hsend[k] = mm(qlt[k], gall[k, y].reshape(256, 128)).astype(BF).reshape(16, 32, 128)
        for dy in far_first:
            for cc in range(2):
                h_copy(k, dy, cc).start()
        for cc in range(2):

            @pl.when(c != cc)
            def _():
                h_copy(k, 0, cc).start()

        hrecv[k, y] = hsend[k, rep]
        own_copy(k).start()

    def ag_part(k, t, s, d):
        return gall.at[k, t] if s < 3 else gall.at[k, t, pl.ds(d * 2, 2)]

    def ag_copy(d, s, k):
        sign = 1 - 2 * d
        ref = ag_part(k, lax.rem(y - sign * s + NY, NY), s, d)
        return remote(ref, ref, s_ag.at[d, s, k], r_ag.at[d, s, k], at_y(y + sign, c))

    def ag_arrival(d, s, k):
        return ag_part(k, lax.rem(y - (1 - 2 * d) * (s + 1) + NY, NY), s, d)

    def sib_copy(i, k):
        ref = ag_arrival(i // 4, i % 4, k)
        return remote(ref, ref, s_sib.at[i, k], r_sib.at[i, k], sib)

    def gather(s, ks):
        @pl.when(jnp.logical_not(active))
        def _():
            for k in ks:
                if s == 0:
                    own_copy(k).wait_recv()
                for d in range(2):
                    if s > 0:
                        ref = ag_arrival(d, s - 1, k)
                        remote(ref, ref, s_ag.at[d, s - 1, k], r_ag.at[d, s - 1, k], sib).wait_recv()
                    if s < 4:
                        ag_copy(d, s, k).start()
                if s > 0:
                    for d in range(2):
                        sib_copy(d * 4 + s - 1, k).start()

    @pl.when(active)
    def _():
        regroup_slot(0)
        regroup_slot(1)
        for k in range(SLOTS):
            if k + 2 < SLOTS:
                regroup_slot(k + 2)
            left_product(k)

    def out_copies(k):
        return [
            pltpu.make_async_copy(o1.at[k], out_1.at[k], s_out.at[0, k]),
            pltpu.make_async_copy(o2.at[k], out_2.at[k], s_out.at[1, k]),
            pltpu.make_async_copy(ol.at[k], out_l.at[k], s_out.at[2, k]),
            pltpu.make_async_copy(orr.at[k], out_r.at[k], s_out.at[3, k]),
        ]

    lane_low = iota((32, 128), 1) < 64
    back = {}

    def slot_products(k):
        for dy in range(1, NY):
            h_wait(k, dy)

        @pl.when(jnp.logical_not(active))
        def _():
            h_wait(k, 0)

        h = jnp.concatenate(
            [(hrecv[k, q].astype(F32) + hrecv[k, q + 4].astype(F32)).astype(BF) for q in range(4)], axis=1
        )
        rotated = mm(h, qr[k].reshape(512, 512))
        first = BETA_FIRST * m1[k] + (1.0 - BETA_FIRST) * rotated
        second = BETA_SECOND * m2[k] + (1.0 - BETA_SECOND) * rotated * rotated
        o1[k] = first
        o2[k] = second
        for copy in out_copies(k)[:2]:
            copy.start()
        direction = (first / (jnp.sqrt(second) + EPSILON)).astype(BF)
        if k in (0, 2, 4):
            back[k, 0] = mm_t(direction, qr[k].reshape(512, 512)).astype(BF)
        if k in (1, 3, 4):
            back[k, 1] = mm_t(direction, qrs[(k - 1) // 2 if k < 4 else 2].reshape(512, 512)).astype(BF)

    def b_copy(p, dy):
        yy = lax.rem(y + dy, NY)
        return remote(bmsg.at[p, yy], bb.at[p, rep], s_b.at[p, dy], r_b.at[p, rep], (yy * 2 + PAIR_CORE[p], own))

    def send_back(p):
        a, b = PAIRS[p]
        for yy in range(NY):
            lanes = slice((yy // 2) * 128, (yy // 2) * 128 + 128)
            lo, hi = back[a, 0][:, lanes], back[b, 1][:, lanes]
            bmsg[p, yy] = jnp.where(lane_low, lo, hi) if yy % 2 == 0 else jnp.where(lane_low, hi, lo)
        for dy in far_first:
            b_copy(p, dy).start()

        @pl.when(c != PAIR_CORE[p])
        def _():
            b_copy(p, 0).start()

        @pl.when(c == PAIR_CORE[p])
        def _():
            bb[p, rep] = bmsg[p, y]

    def stat_products(k):
        @pl.when(active)
        def _():
            for i in range(8):
                ref = ag_arrival(i // 4, i % 4, k)
                remote(ref, ref, s_sib.at[i, k], r_sib.at[i, k], sib).wait_recv()

        for t in range(NY):
            gf[pl.ds((t // 4) * 256, 256), pl.ds((t % 4) * 128, 128)] = gall[k, t].reshape(256, 128)
        columns = mm_t(mine, gf[...]).astype(BF)
        right = mm(columns, gf[...])
        orr[k] = (BETA_SECOND * sr[k].astype(F32) + (1.0 - BETA_SECOND) * right).astype(BF)
        rows = mm(pm[pl.ds(pl.multiple_of(rep * 32, 32), 32), :], gf[...]).astype(BF)
        left = mm_t(rows, gf[...])
        high = left.astype(BF)
        low = (left - high.astype(F32)).astype(BF)
        left = mm_t(high, pm[...]) + mm_t(low, pm[...])
        ol[k] = (BETA_SECOND * sl[k].astype(F32) + (1.0 - BETA_SECOND) * left).astype(BF)
        for copy in out_copies(k)[2:]:
            copy.start()

    def z2_copy(p, j):
        to = lax.rem(z + j, NZ)
        if p == 2:
            src, dst = ub4.at[to], w24.at[z]
        else:
            src, dst = ub.at[p, pl.ds(pl.multiple_of(to * 32, 32), 32)], w2.at[p, z]
        return remote(src, dst, s_z2.at[p, j - 1], r_z2.at[p, z], at_z(to))

    def z2_wait(p, j):
        src = lax.rem(z + j, NZ)
        a, b = (ub4.at[0], w24.at[src]) if p == 2 else (ub.at[p, pl.ds(0, 32)], w2.at[p, src])
        remote(a, b, s_z2.at[p, 0], r_z2.at[p, src], at_z(src)).wait_recv()

    def x2_copy(p, j):
        to = lax.rem(x + j, NX)
        part = lax.rem(to, 2) if p == 2 else to
        return remote(xs2.at[p, part], yb.at[p, x], s_x2.at[p, j - 1], r_x2.at[p, x], at_x(to))

    def y_copy(p):
        return remote(yb.at[p], yb.at[p], s_y.at[p], r_y.at[p], sib)

    def update_products(p):
        for d in range(1, 16):
            src = lax.rem(rep + d, 16)
            remote(bmsg.at[p, 0], bb.at[p, src], s_b.at[p, 0], r_b.at[p, src], (src, own)).wait_recv()
        a, b = PAIRS[p]
        columns = bb[p].reshape(512, 128)
        if p == 2:
            whole = mm(ql[a], columns).astype(BF).reshape(NZ, 2, 16, 128)
            low = iota((NZ, 16, 128), 2) < 64
            ub4[...] = jnp.where(low, whole[:, 0], whole[:, 1])
        else:
            swap = jnp.where(iota((512, 128), 1) < 64, 0, 1) == (y & 1)
            ub[p] = jnp.where(swap, mm(ql[a], columns), mm(ql[b], columns)).astype(BF)
        for j in (8, 7, 9, 6, 10, 5, 11, 4, 12, 3, 13, 2, 14, 1, 15):
            z2_copy(p, j).start()
        if p == 2:
            w24[z] = ub4[z]
        else:
            w2[p, z] = ub[p, pl.ds(pl.multiple_of(z * 32, 32), 32)]

    def update_regroup(p):
        for j in range(1, NZ):
            z2_wait(p, j)
        if p == 2:
            parts = mm(perm4[...], w24[...].reshape(256, 128)).astype(BF).reshape(2, 8, 16, 128)
            xs2[p, pl.ds(0, 2)] = parts
        else:
            xs2[p] = mm(perm3[...], w2[p].reshape(512, 128)).astype(BF).reshape(NX, 8, 16, 128)
        for j in (2, 1, 3):
            x2_copy(p, j).start()
        yb[p, x] = xs2[p, lax.rem(x, 2) if p == 2 else x]

    def update_share(p):
        for j in range(1, NX):
            src = lax.rem(x + j, NX)
            remote(xs2.at[p, 0], yb.at[p, src], s_x2.at[p, 0], r_x2.at[p, src], at_x(src)).wait_recv()
        y_copy(p).start()

    slot_products(0)
    gather(0, (0, 1, 2))
    slot_products(1)
    send_back(0)
    gather(0, (3, 4))
    slot_products(2)
    slot_products(3)
    send_back(1)
    gather(1, (0, 1))
    slot_products(4)
    send_back(2)
    gather(1, (2, 3, 4))
    j3 = iota((512, 1), 0)
    perm3[...] = onehot(iota((512, 512), 1), (j3 & 15) * 32 + (j3 >> 7) * 8 + ((j3 >> 4) & 7))
    perm4[...] = onehot(iota((256, 256), 1), (j2 & 15) * 16 + (j2 >> 7) * 8 + ((j2 >> 4) & 7))
    oh2[...] = onehot(iota((512, PADB), 0), slot_code)
    yb[pl.ds(3, 1)] = jnp.zeros((1, NX, 8, 16, 128), BF)

    def on_core(core, steps):
        @pl.when(c == core)
        def _():
            for step, p in steps:
                step(p)

    on_core(0, [(update_products, 0)])
    gather(2, (0, 1, 2, 3, 4))
    on_core(0, [(update_products, 2), (update_regroup, 0)])
    on_core(1, [(update_products, 1)])
    gather(3, (0, 1, 2, 3, 4))
    on_core(0, [(update_share, 0)])
    on_core(1, [(update_regroup, 1)])
    gather(4, (0, 1))
    stat_products(0)
    stat_products(1)
    gather(4, (2, 3, 4))
    on_core(0, [(update_regroup, 2)])
    on_core(1, [(update_share, 1)])
    stat_products(2)
    stat_products(3)
    on_core(0, [(update_share, 2)])
    stat_products(4)

    @pl.when(c == 0)
    def _():
        y_copy(1).wait_recv()

    @pl.when(c == 1)
    def _():
        y_copy(0).wait_recv()
        y_copy(2).wait_recv()

    chosen = onehot(
        iota((64, 128), 1), (iota((64, 1), 0) >> 5) * 64 + 32 * c + (iota((64, 1), 0) & 31)
    )
    for i in range(8):
        lanes = mm_t(chosen, yb[:, :, i].reshape(256, 128)).astype(BF)
        wbuf[pl.ds(i * 32, 32), pl.ds(0, 256)] = lanes[:32]
        wbuf[pl.ds(i * 32, 32), pl.ds(256, 256)] = lanes[32:]
    out_u[...] = mm(wbuf[...], oh2[...]).astype(BF)[:, :NB]

    def drain_4():
        @pl.when(active)
        def _():
            for k in range(SLOTS):
                for dy in far_first:
                    for cc in range(2):
                        h_copy(k, dy, cc).wait_send()
                for cc in range(2):

                    @pl.when(c != cc)
                    def _():
                        h_copy(k, 0, cc).wait_send()

                own_copy(k).wait_send()

        @pl.when(jnp.logical_not(active))
        def _():
            for k in range(SLOTS):
                for s in range(4):
                    for d in range(2):
                        ag_copy(d, s, k).wait_send()
                        sib_copy(d * 4 + s, k).wait_send()

        for p in range(3):
            for dy in far_first:
                b_copy(p, dy).wait_send()

            @pl.when(c != PAIR_CORE[p])
            def _():
                b_copy(p, 0).wait_send()

            @pl.when(c == PAIR_CORE[p])
            def _():
                for j in range(1, NZ):
                    z2_copy(p, j).wait_send()
                for j in range(1, NX):
                    x2_copy(p, j).wait_send()
                y_copy(p).wait_send()

    drains.append(drain_4)
    for k in range(SLOTS):
        for copy in out_copies(k):
            copy.wait()
    for drain in drains:
        drain()


def onehot_lt(a, b):
    return jnp.where(a < b, 1.0, 0.0).astype(BF)


def hand_on(*refs):
    count = len(refs) // 2
    for i in range(count):
        refs[count + i][...] = refs[i][...]


def shards(grad_parts, owner_of, stats_left, stats_right, basis_left, basis_right, moment_first, moment_second):
    blocks = owner_of.shape[0]
    padded = jnp.pad(owner_of[:, 0], (0, PADB - blocks), constant_values=-1)
    anywhere = pl.BlockSpec(memory_space=pl.ANY)
    vmem = pl.BlockSpec(memory_space=pltpu.VMEM)
    rows = (SLOTS, 32, 512)
    dma = pltpu.SemaphoreType.DMA
    scratch = [
        pltpu.VMEM((1152, 256), BF),
        pltpu.VMEM((1152, 256), BF),
        pltpu.VMEM((4, NB, 512), BF),
        pltpu.VMEM((2, 4, NB, 512), BF),
        pltpu.VMEM((2, 3, NB, 512), BF),
        pltpu.VMEM((PADB, 512), BF),
        pltpu.VMEM((4, 640, PADB), BF),
        pltpu.VMEM((SLOTS, 8, 16, 128), BF),
        pltpu.VMEM((SLOTS, NZ, 16, 128), BF),
        pltpu.VMEM((SLOTS, NX, 4, 16, 128), BF),
        pltpu.VMEM((SLOTS, NY, 4, 64, 128), BF),
        pltpu.VMEM((SLOTS, 512, 512), BF),
        pltpu.VMEM((SLOTS, 4, 2, 64, 512), BF),
        pltpu.VMEM((3, 4, 2, 64, 512), BF),
        pltpu.VMEM(rows, BF),
        pltpu.VMEM(rows, BF),
        pltpu.VMEM(rows, F32),
        pltpu.VMEM(rows, F32),
        pltpu.VMEM(rows, BF),
        pltpu.VMEM(rows, BF),
        pltpu.VMEM(rows, F32),
        pltpu.VMEM(rows, F32),
        pltpu.VMEM((SLOTS, 512, 256), BF),
        pltpu.VMEM((SLOTS, 16, 32, 128), BF),
        pltpu.VMEM((SLOTS, NY, 32, 128), BF),
        pltpu.VMEM((512, 512), BF),
        pltpu.VMEM((512, 512), BF),
        pltpu.VMEM((256, 256), BF),
        pltpu.VMEM((512, 512), BF),
        pltpu.VMEM((256, 256), BF),
        pltpu.VMEM((512, PADB), BF),
        pltpu.VMEM((256, 512), BF),
        pltpu.VMEM((3, NY, 32, 128), BF),
        pltpu.VMEM((3, 16, 32, 128), BF),
        pltpu.VMEM((2, 512, 128), BF),
        pltpu.VMEM((NZ, 16, 128), BF),
        pltpu.VMEM((2, NZ, 32, 128), BF),
        pltpu.VMEM((NZ, 16, 128), BF),
        pltpu.VMEM((3, NX, 8, 16, 128), BF),
        pltpu.VMEM((4, NX, 8, 16, 128), BF),
        dma((13,)),
        dma((4, SLOTS)),
        dma((3,)), dma((3,)),
        dma((2, 4, SUBS)), dma((2, 4, SUBS)),
        dma((SUBS,)), dma((SUBS,)),
        dma((SLOTS, 8)), dma((SLOTS, NZ)),
        dma((SLOTS, 3)), dma((SLOTS, NX)),
        dma((SLOTS, NY, 2)), dma((SLOTS, NY)),
        dma((SLOTS,)), dma((SLOTS,)),
        dma((2, 4, SLOTS)), dma((2, 4, SLOTS)),
        dma((8, SLOTS)), dma((8, SLOTS)),
        dma((3, NY)), dma((3, 16)),
        dma((3, NZ - 1)), dma((3, NZ)),
        dma((3, NX - 1)), dma((3, NX)),
        dma((3,)), dma((3,)),
    ]
    shapes = (
        jax.ShapeDtypeStruct(rows, BF),
        jax.ShapeDtypeStruct(rows, BF),
        jax.ShapeDtypeStruct(rows, F32),
        jax.ShapeDtypeStruct(rows, F32),
        jax.ShapeDtypeStruct((256, blocks), BF),
    )
    results = pl.pallas_call(
        kernel,
        out_shape=shapes,
        in_specs=[anywhere, vmem] + [anywhere] * 6,
        out_specs=(anywhere,) * 4 + (vmem,),
        scratch_shapes=scratch,
        compiler_params=pltpu.CompilerParams(
            collective_id=0, has_side_effects=True, vmem_limit_bytes=56 * 1024 * 1024
        ),
    )(
        grad_parts[0].reshape(blocks * 8, 512),
        padded[None, :],
        stats_left[0],
        stats_right[0],
        basis_left[0],
        basis_right[0].reshape(SLOTS, 4, 2, 64, 512),
        moment_first[0],
        moment_second[0],
    )
    new_left, new_right, new_first, new_second, picked = pl.pallas_call(
        hand_on,
        out_shape=shapes,
        in_specs=[vmem] * 5,
        out_specs=(vmem,) * 5,
    )(*results)
    update = picked.reshape(8, 32, blocks).transpose(2, 0, 1)
    return (new_left[None], new_right[None], new_first[None], new_second[None], update)


def solution(mesh):
    return jax.shard_map(
        shards,
        mesh=mesh,
        in_specs=(
            P("replica", None, "owner", None),
            P(),
            P("owner", None, "replica", None),
            P("owner", None, "replica", None),
            P("owner", None, None, None),
            P("owner", None, None, None),
            P("owner", None, "replica", None),
            P("owner", None, "replica", None),
        ),
        out_specs=(
            P("owner", None, "replica", None),
            P("owner", None, "replica", None),
            P("owner", None, "replica", None),
            P("owner", None, "replica", None),
            P(None, "owner", "replica"),
        ),
        check_vma=False,
    )
```

```python
import jax
import jax.numpy as jnp
from jax import lax
from jax.experimental import pallas as pl
from jax.experimental.pallas import tpu as pltpu
from jax.sharding import PartitionSpec as P

BETA_FIRST = 0.9
BETA_SECOND = 0.95
EPSILON = 1e-08
MESH = pl.DeviceIdType.MESH
BF = jnp.bfloat16
F32 = jnp.float32
NY, NX, NZ = 8, 4, 16
NB, PADB = 144, 256
SLOTS = 5
SUBS, SUBROWS = 3, 48
PAIRS = ((0, 1), (2, 3), (4, 4))
PAIR_CORE = (0, 1, 0)


def mm(a, b):
    return jnp.dot(a, b, preferred_element_type=F32)


def mm_t(a, b):
    return lax.dot_general(a, b, (((1,), (1,)), ((), ())), preferred_element_type=F32)


def iota(shape, axis):
    return lax.broadcasted_iota(jnp.int32, shape, axis)


def onehot(a, b):
    return jnp.where(a == b, 1.0, 0.0).astype(BF)


def kernel(
    grad, own_row, stats_l, stats_r, basis_l, basis_r, mom1, mom2,
    out_l, out_r, out_1, out_2, out_u,
    go, gx, chunk, rs_mid, rs_end, rs_send, summed, place, v1, w1, xs1, gall,
    ql, qr, qrs, sl, sr, m1, m2, ol, orr, o1, o2, qlt, hsend, hrecv, gf, pm, perm2, perm3, perm4, oh2, wbuf,
    bmsg, bb, ub, ub4, w2, w24, xs2, yb,
    s_in, s_out, s_core, r_core, s_rs, r_mid, r_end, s_cag, r_cag, s_z1, r_z1, s_x1, r_x1,
    s_h, r_h, s_own, r_own, s_ag, r_ag, s_sib, r_sib, s_b, r_b, s_z2, r_z2, s_x2, r_x2, s_y, r_y,
):
    rep = lax.axis_index("replica")
    own = lax.axis_index("owner")
    y, c = rep // 2, rep % 2
    z, x = own // NX, own % NX
    sib = (y * 2 + (1 - c), own)
    zhalf = z // 8
    active = c == zhalf

    def at_y(yy, cc):
        return (lax.rem(yy + 2 * NY, NY) * 2 + cc, own)

    def at_z(zz):
        return (rep, zz * NX + x)

    def at_x(xx):
        return (rep, z * NX + xx)

    def remote(src, dst, ssem, rsem, dev):
        return pltpu.make_async_remote_copy(
            src_ref=src, dst_ref=dst, send_sem=ssem, recv_sem=rsem, device_id=dev, device_id_type=MESH
        )

    def received(ref, sem):
        remote(ref, ref, sem, sem, sib).wait_recv()

    def sent(ref, sem):
        remote(ref, ref, sem, sem, sib).wait_send()

    half = pl.ds(pl.multiple_of(c * 256, 256), 256)
    other = pl.ds(pl.multiple_of((1 - c) * 256, 256), 256)
    loads = [pltpu.make_async_copy(grad.at[:, half], go, s_in.at[0])]
    loads += [
        pltpu.make_async_copy(src, dst, s_in.at[1 + i])
        for i, (src, dst) in enumerate(
            ((basis_l, ql), (basis_r, qr), (stats_l, sl), (stats_r, sr), (mom1, m1), (mom2, m2))
        )
    ]
    swaps = [
        pltpu.make_async_copy(basis_r.at[k, :, h], qrs.at[i, :, 1 - h], s_in.at[7])
        for i, k in enumerate((1, 3, 4))
        for h in range(2)
    ]
    loads[0].start()
    drains = []

    barrier = pltpu.get_barrier_semaphore()
    for d in range(1, 16):
        pl.semaphore_signal(barrier, inc=1, device_id=(lax.rem(rep + d, 16), own), device_id_type=MESH)
    for d in range(1, NZ):
        pl.semaphore_signal(barrier, inc=1, device_id=at_z(lax.rem(z + d, NZ)), device_id_type=MESH)
    for d in range(1, NX):
        for cc in range(2):
            to = (y * 2 + cc, z * NX + lax.rem(x + d, NX))
            pl.semaphore_signal(barrier, inc=1, device_id=to, device_id_type=MESH)
    pl.semaphore_wait(barrier, 15 + NZ - 1 + 2 * (NX - 1))

    def core_copy(j):
        rows = pl.ds(j * 384, 384)
        return remote(grad.at[rows, other], gx.at[rows], s_core.at[0], r_core.at[j], sib)

    def rs_target(step):
        t = lax.rem(y + step + NY, NY)
        return (t // 4) * 2 + t % 2, c == (t % 4) // 2

    def rs_copy(d, step, j):
        sign = 1 - 2 * d
        rows = pl.ds(j * SUBROWS, SUBROWS)
        which = rs_target(sign * step)[0]
        if step == 4:
            lanes = pl.ds(d * 256, 256)
            src, dst = chunk.at[which, rows, lanes], rs_mid.at[d, 0, rows, lanes]
            sem, to = r_mid.at[d, 0, j], y + 2 * sign
        elif step == 3:
            src, dst = chunk.at[which, rows], rs_mid.at[d, 1, rows]
            sem, to = r_mid.at[d, 1, j], y + sign
        elif step == 2:
            src, dst = rs_send.at[d, rows], rs_end.at[d, 1, rows]
            sem, to = r_end.at[j], y + 2 * sign
        else:
            src, dst = chunk.at[which, rows], rs_end.at[d, 0, rows]
            sem, to = r_end.at[j], y + sign
        return remote(src, dst, s_rs.at[0], sem, at_y(to, c))

    def rs_start(step, j):
        for d in range(2):

            @pl.when(rs_target((1 - 2 * d) * step)[1])
            def _():
                rs_copy(d, step, j).start()

    for j in range(3):
        core_copy(j).start()
    for d in loads[1:] + swaps:
        d.start()

    out_of = iota((128, 1), 0)
    perm1 = onehot(iota((128, 128), 1), (out_of % 16) * 8 + out_of // 16)
    o_row = own_row[...]
    e_row = onehot(iota((128, PADB), 0), o_row)
    before = mm(e_row, onehot_lt(iota((PADB, PADB), 0), iota((PADB, PADB), 1)))
    k_row = jnp.sum(before * e_row.astype(F32), axis=0, keepdims=True).astype(jnp.int32)
    zr, xr = o_row >> 2, o_row & 3
    code = jnp.where((zr >> 3) == c, (k_row * 8 + (zr & 7)) * 16 + xr, -64)
    for q in range(4):
        place[q] = onehot(iota((640, PADB), 0), code + 4 * q)
    side = jnp.where(k_row == 4, x >> 1, (k_row + y) & 1)
    slot_code = side * 256 + (k_row >> 1) * 64 + xr * 16 + zr
    summed[pl.ds(NB, PADB - NB), :] = jnp.zeros((PADB - NB, 512), BF)

    loads[0].wait()
    for j in range(3):
        core_copy(j).wait_recv()
        for g in range(3 * j, 3 * j + 3):
            rows = pl.ds(g * 128, 128)
            both = (mm(perm1, go[rows, :]) + mm(perm1, gx[rows, :])).astype(BF)
            for i in range(8):
                for q in range(2):
                    chunk[(i // 4) * 2 + q, pl.ds(g * 16, 16), pl.ds((i % 4) * 128, 128)] = both[
                        i * 16 : i * 16 + 16, q * 128 : q * 128 + 128
                    ]

        rs_start(4, j)
        rs_start(3, j)
    drains.append(lambda: sent(gx, s_core.at[0]))
    for j in range(SUBS):
        rs_start(1, j)

    for d in loads[1:]:
        d.wait()
    pltpu.make_async_copy(qrs, qrs, s_in.at[7]).wait()
    r_col = iota((256, 1), 0)
    held = ((r_col & 15) * 4 + ((r_col >> 4) & 3)) * 8 + (y // 4) * 4 + (r_col >> 6)
    held_rows = onehot(iota((256, 512), 1), held)
    same = onehot(iota((512, 512), 0), iota((512, 512), 1))

    def turn_basis(k):
        qlt[k] = mm_t(same, mm(held_rows, ql[k]).astype(BF)).astype(BF)

    turn_basis(0)
    turn_basis(1)
    turn_basis(2)

    for j in range(SUBS):
        for d in range(2):
            rows = pl.ds(j * SUBROWS, SUBROWS)
            t, here = rs_target((1 - 2 * d) * 2)

            @pl.when(here)
            def _():
                lanes = pl.ds(d * 256, 256)
                rest = pl.ds((1 - d) * 256, 256)
                received(rs_mid.at[d, 0, rows, lanes], r_mid.at[d, 0, j])
                received(rs_mid.at[d, 1, rows], r_mid.at[d, 1, j])
                rs_send[d, rows, lanes] = (
                    chunk[t, rows, lanes].astype(F32)
                    + rs_mid[d, 0, rows, lanes].astype(F32)
                    + rs_mid[d, 1, rows, lanes].astype(F32)
                ).astype(BF)
                rs_send[d, rows, rest] = (
                    chunk[t, rows, rest].astype(F32) + rs_mid[d, 1, rows, rest].astype(F32)
                ).astype(BF)
                rs_copy(d, 2, j).start()

    turn_basis(3)
    turn_basis(4)
    j2 = iota((256, 1), 0)
    perm2[...] = onehot(iota((256, 256), 1), (j2 & 15) * 16 + ((j2 >> 4) & 3) * 4 + (j2 >> 6))
    rho = iota((1, 512), 1)
    natural = ((rho & 15) * 4 + ((rho >> 4) & 3)) * 8 + (rho >> 8) * 4 + ((rho >> 6) & 3)
    pm[...] = onehot(iota((512, 512), 0), natural)
    last, sums_here = rs_target(0)
    sums = summed.at[pl.ds(0, NB)]

    @pl.when(sums_here)
    def _():
        for j in range(SUBS):
            rows = pl.ds(j * SUBROWS, SUBROWS)
            received(rs_end.at[:, :, rows], r_end.at[j])
            total = chunk[last, rows].astype(F32)
            for d in range(2):
                total += rs_end[d, 0, rows].astype(F32) + rs_end[d, 1, rows].astype(F32)
            summed[rows] = total.astype(BF)
            ref = summed.at[rows]
            remote(ref, ref, s_cag.at[0], r_cag.at[0], sib).start()

    @pl.when(jnp.logical_not(sums_here))
    def _():
        received(sums, r_cag.at[0])

    def drain_2():
        @pl.when(sums_here)
        def _():
            sent(chunk.at[pl.ds(0, 3)], s_rs.at[0])
            sent(sums, s_cag.at[0])

        @pl.when(jnp.logical_not(sums_here))
        def _():
            sent(chunk, s_rs.at[0])

    drains.append(drain_2)

    def z1_copy(k, j):
        low = lax.rem(z + j + 4 * active.astype(jnp.int32), 8)
        return remote(v1.at[k, low], w1.at[k, z], s_z1.at[0], r_z1.at[k], at_z(c * 8 + low))

    def fill_slots(k, n):
        rows = pl.ds(k * 128, n * 128)
        placed = mm(place[0, rows], summed[:, pl.ds(0, 128)])
        for q in range(1, 4):
            placed += mm(place[q, rows], summed[:, pl.ds(q * 128, 128)])
        v1[pl.ds(k, n)] = placed.astype(BF).reshape(n, 8, 16, 128)
        for kk in range(k, k + n):
            for j in (0, 1, 7, 2, 6, 3, 5):
                z1_copy(kk, j).start()

            @pl.when(jnp.logical_not(active))
            def _():
                z1_copy(kk, 4).start()

        @pl.when(active)
        def _():
            w1[pl.ds(k, n), z] = v1[pl.ds(k, n), lax.rem(z, 8)]

    fill_slots(0, 1)
    fill_slots(1, 4)

    def drain_3():
        @pl.when(jnp.logical_not(active))
        def _():
            sent(v1, s_z1.at[0])

        @pl.when(active)
        def _():
            sent(v1.at[:, pl.ds(0, 7)], s_z1.at[0])
            sent(xs1.at[:, pl.ds(0, NX - 1)], s_x1.at[0])

    drains.append(drain_3)

    mine = onehot(iota((32, 512), 1), iota((32, 512), 0) + rep * 32)

    def x1_copy(k, j):
        to = lax.rem(x + j, NX)
        rows = pl.ds(pl.multiple_of(x * 16, 16), 16)
        return remote(xs1.at[k, to], gall.at[k, y, :, rows], s_x1.at[0], r_x1.at[k], at_x(to))

    def regroup_slot(k):
        received(w1.at[k, pl.ds(0, NZ - 1)], r_z1.at[k])
        xs1[k] = mm(perm2[...], w1[k].reshape(256, 128)).astype(BF).reshape(NX, 4, 16, 128)
        for j in (2, 1, 3):
            x1_copy(k, j).start()
        gall[k, y, :, pl.ds(pl.multiple_of(x * 16, 16), 16)] = xs1[k, x]

    def h_copy(k, dy, cc):
        to = lax.rem(y + dy, NY) * 2 + cc
        return remote(hsend.at[k, to], hrecv.at[k, y], s_h.at[0], r_h.at[k], (to, own))

    def own_copy(k):
        ref = gall.at[k, y]
        return remote(ref, ref, s_own.at[0], r_own.at[k], sib)

    far_first = (4, 3, 5, 2, 6, 1, 7)

    def left_product(k):
        received(xs1.at[k, pl.ds(0, NX - 1)], r_x1.at[k])
        hsend[k] = mm(qlt[k], gall[k, y].reshape(256, 128)).astype(BF).reshape(16, 32, 128)
        for dy in far_first:
            for cc in range(2):
                h_copy(k, dy, cc).start()
        for cc in range(2):

            @pl.when(c != cc)
            def _():
                h_copy(k, 0, cc).start()

        hrecv[k, y] = hsend[k, rep]
        own_copy(k).start()

    groups = ((0, 2), (2, 3))

    def ag_part(g, t, s, d):
        ks = pl.ds(*groups[g])
        return gall.at[ks, t] if s < 3 else gall.at[ks, t, pl.ds(d * 2, 2)]

    def ag_copy(d, s, g):
        sign = 1 - 2 * d
        ref = ag_part(g, lax.rem(y - sign * s + NY, NY), s, d)
        return remote(ref, ref, s_ag.at[0], r_ag.at[d, s, g], at_y(y + sign, c))

    def ag_arrival(d, s, g):
        return ag_part(g, lax.rem(y - (1 - 2 * d) * (s + 1) + NY, NY), s, d)

    def gather(s, g):
        @pl.when(jnp.logical_not(active))
        def _():
            if s == 0:
                for k in range(groups[g][0], sum(groups[g])):
                    received(gall.at[k, y], r_own.at[k])
            for d in range(2):
                if s > 0:
                    received(ag_arrival(d, s - 1, g), r_ag.at[d, s - 1, g])
                if s < 4:
                    ag_copy(d, s, g).start()
            if s > 0:
                for d in range(2):
                    ref = ag_arrival(d, s - 1, g)
                    remote(ref, ref, s_sib.at[0], r_sib.at[g], sib).start()

    @pl.when(active)
    def _():
        regroup_slot(0)
        regroup_slot(1)
        for k in range(SLOTS):
            if k + 2 < SLOTS:
                regroup_slot(k + 2)
            left_product(k)

    def out_copies(k):
        return [
            pltpu.make_async_copy(src.at[k], dst.at[k], s_out.at[i])
            for i, (src, dst) in enumerate(((o1, out_1), (o2, out_2), (ol, out_l), (orr, out_r)))
        ]

    lane_low = iota((32, 128), 1) < 64
    back = {}

    def slot_products(k):
        @pl.when(active)
        def _():
            received(hrecv.at[k, pl.ds(0, NY - 1)], r_h.at[k])

        @pl.when(jnp.logical_not(active))
        def _():
            received(hrecv.at[k], r_h.at[k])

        h = jnp.concatenate(
            [(hrecv[k, q].astype(F32) + hrecv[k, q + 4].astype(F32)).astype(BF) for q in range(4)], axis=1
        )
        rotated = mm(h, qr[k].reshape(512, 512))
        first = BETA_FIRST * m1[k] + (1.0 - BETA_FIRST) * rotated
        second = BETA_SECOND * m2[k] + (1.0 - BETA_SECOND) * rotated * rotated
        o1[k] = first
        o2[k] = second
        for copy in out_copies(k)[:2]:
            copy.start()
        direction = (first / (jnp.sqrt(second) + EPSILON)).astype(BF)
        if k in (0, 2, 4):
            back[k, 0] = mm_t(direction, qr[k].reshape(512, 512)).astype(BF)
        if k in (1, 3, 4):
            back[k, 1] = mm_t(direction, qrs[(k - 1) // 2 if k < 4 else 2].reshape(512, 512)).astype(BF)

    def b_copy(p, dy):
        yy = lax.rem(y + dy, NY)
        return remote(bmsg.at[p, yy], bb.at[p, rep], s_b.at[p], r_b.at[p], (yy * 2 + PAIR_CORE[p], own))

    def send_back(p):
        a, b = PAIRS[p]
        for yy in range(NY):
            lanes = slice((yy // 2) * 128, (yy // 2) * 128 + 128)
            lo, hi = back[a, 0][:, lanes], back[b, 1][:, lanes]
            bmsg[p, yy] = jnp.where(lane_low, lo, hi) if yy % 2 == 0 else jnp.where(lane_low, hi, lo)
        for dy in far_first:
            b_copy(p, dy).start()

        @pl.when(c != PAIR_CORE[p])
        def _():
            b_copy(p, 0).start()

        @pl.when(c == PAIR_CORE[p])
        def _():
            bb[p, rep] = bmsg[p, y]

    def stat_products(k):
        for g in range(2):
            if k == groups[g][0]:

                @pl.when(active)
                def _():
                    received(gall.at[pl.ds(*groups[g]), pl.ds(0, NY - 1)], r_sib.at[g])

        for t in range(NY):
            gf[pl.ds((t // 4) * 256, 256), pl.ds((t % 4) * 128, 128)] = gall[k, t].reshape(256, 128)
        columns = mm_t(mine, gf[...]).astype(BF)
        right = mm(columns, gf[...])
        orr[k] = (BETA_SECOND * sr[k].astype(F32) + (1.0 - BETA_SECOND) * right).astype(BF)
        rows = mm(pm[pl.ds(pl.multiple_of(rep * 32, 32), 32), :], gf[...]).astype(BF)
        left = mm_t(rows, gf[...])
        high = left.astype(BF)
        low = (left - high.astype(F32)).astype(BF)
        left = mm_t(high, pm[...]) + mm_t(low, pm[...])
        ol[k] = (BETA_SECOND * sl[k].astype(F32) + (1.0 - BETA_SECOND) * left).astype(BF)
        for copy in out_copies(k)[2:]:
            copy.start()

    def z2_copy(p, j):
        to = lax.rem(z + j, NZ)
        if p == 2:
            src, dst = ub4.at[to], w24.at[z]
        else:
            src, dst = ub.at[p, pl.ds(pl.multiple_of(to * 32, 32), 32)], w2.at[p, z]
        return remote(src, dst, s_z2.at[p], r_z2.at[p], at_z(to))

    def x2_copy(p, j, cc):
        to = lax.rem(x + j, NX)
        part = lax.rem(to, 2) if p == 2 else to
        return remote(xs2.at[p, part], yb.at[p, x], s_x2.at[p], r_x2.at[p], (y * 2 + cc, z * NX + to))

    def y_copy(p):
        return remote(yb.at[p], yb.at[p], s_y.at[p], r_y.at[p], sib)

    def update_products(p):
        received(bb.at[p, pl.ds(0, 15)], r_b.at[p])
        a, b = PAIRS[p]
        columns = bb[p].reshape(512, 128)
        if p == 2:
            whole = mm(ql[a], columns).astype(BF).reshape(NZ, 2, 16, 128)
            low = iota((NZ, 16, 128), 2) < 64
            ub4[...] = jnp.where(low, whole[:, 0], whole[:, 1])
        else:
            swap = jnp.where(iota((512, 128), 1) < 64, 0, 1) == (y & 1)
            ub[p] = jnp.where(swap, mm(ql[a], columns), mm(ql[b], columns)).astype(BF)
        for j in (8, 7, 9, 6, 10, 5, 11, 4, 12, 3, 13, 2, 14, 1, 15):
            z2_copy(p, j).start()
        if p == 2:
            w24[z] = ub4[z]
        else:
            w2[p, z] = ub[p, pl.ds(pl.multiple_of(z * 32, 32), 32)]

    def update_regroup(p):
        if p == 2:
            received(w24.at[pl.ds(0, NZ - 1)], r_z2.at[p])
            parts = mm(perm4[...], w24[...].reshape(256, 128)).astype(BF).reshape(2, 8, 16, 128)
            xs2[p, pl.ds(0, 2)] = parts
            for j in (2, 1, 3, 0):
                for cc in (1, 0)[: 1 + (j > 0)]:
                    x2_copy(p, j, cc).start()
            yb[p, x] = xs2[p, lax.rem(x, 2)]
        else:
            received(w2.at[p, pl.ds(0, NZ - 1)], r_z2.at[p])
            xs2[p] = mm(perm3[...], w2[p].reshape(512, 128)).astype(BF).reshape(NX, 8, 16, 128)
            for j in (2, 1, 3):
                x2_copy(p, j, PAIR_CORE[p]).start()
            yb[p, x] = xs2[p, x]

    def update_share(p):
        received(yb.at[p, pl.ds(0, NX - 1)], r_x2.at[p])
        if p != 2:
            y_copy(p).start()

    slot_products(0)
    gather(0, 0)
    slot_products(1)
    send_back(0)
    slot_products(2)
    gather(0, 1)
    slot_products(3)
    send_back(1)
    gather(1, 0)
    slot_products(4)
    send_back(2)
    j3 = iota((512, 1), 0)
    perm3[...] = onehot(iota((512, 512), 1), (j3 & 15) * 32 + (j3 >> 7) * 8 + ((j3 >> 4) & 7))
    perm4[...] = onehot(iota((256, 256), 1), (j2 & 15) * 16 + (j2 >> 7) * 8 + ((j2 >> 4) & 7))
    oh2[...] = onehot(iota((512, PADB), 0), slot_code)
    yb[pl.ds(3, 1)] = jnp.zeros((1, NX, 8, 16, 128), BF)
    gather(1, 1)

    def on_core(core, step, p):
        @pl.when(c == core)
        def _():
            step(p)

    on_core(0, update_products, 0)
    gather(2, 0)
    on_core(1, update_products, 1)
    gather(2, 1)
    on_core(0, update_products, 2)
    on_core(0, update_regroup, 0)
    gather(3, 0)
    gather(3, 1)
    on_core(1, update_regroup, 1)
    on_core(0, update_share, 0)
    gather(4, 0)
    stat_products(0)
    stat_products(1)
    gather(4, 1)
    on_core(1, update_share, 1)
    on_core(0, update_regroup, 2)
    stat_products(2)
    stat_products(3)
    stat_products(4)

    @pl.when(c == 0)
    def _():
        update_share(2)
        received(yb.at[1], r_y.at[1])

    @pl.when(c == 1)
    def _():
        received(yb.at[0], r_y.at[0])
        received(yb.at[2], r_x2.at[2])

    chosen = onehot(
        iota((64, 128), 1), (iota((64, 1), 0) >> 5) * 64 + 32 * c + (iota((64, 1), 0) & 31)
    )
    for i in range(8):
        lanes = mm_t(chosen, yb[:, :, i].reshape(256, 128)).astype(BF)
        wbuf[pl.ds(i * 32, 32), pl.ds(0, 256)] = lanes[:32]
        wbuf[pl.ds(i * 32, 32), pl.ds(256, 256)] = lanes[32:]
    out_u[...] = mm(wbuf[...], oh2[...]).astype(BF)[:, :NB]

    def drain_4():
        @pl.when(active)
        def _():
            sent(hsend.at[:, pl.ds(0, 15)], s_h.at[0])
            sent(gall.at[:, 0], s_own.at[0])

        @pl.when(jnp.logical_not(active))
        def _():
            sent(gall.at[:, pl.ds(0, 7)], s_ag.at[0])
            sent(gall.at[:, pl.ds(0, 7)], s_sib.at[0])

        for p in range(3):

            @pl.when(c != PAIR_CORE[p])
            def _():
                sent(bmsg.at[p], s_b.at[p])

            @pl.when(c == PAIR_CORE[p])
            def _():
                sent(bmsg.at[p, pl.ds(0, 7)], s_b.at[p])
                if p == 2:
                    sent(ub4.at[pl.ds(0, NZ - 1)], s_z2.at[p])
                    sent(gall.at[0, pl.ds(0, 7), pl.ds(0, 2)], s_x2.at[p])
                else:
                    sent(w2.at[p, pl.ds(0, NZ - 1)], s_z2.at[p])
                    sent(yb.at[p, pl.ds(0, NX - 1)], s_x2.at[p])
                    sent(yb.at[p], s_y.at[p])

    drains.append(drain_4)
    for i, (src, dst) in enumerate(((o1, out_1), (o2, out_2), (ol, out_l), (orr, out_r))):
        pltpu.make_async_copy(src, dst, s_out.at[i]).wait()
    for drain in drains:
        drain()


def onehot_lt(a, b):
    return jnp.where(a < b, 1.0, 0.0).astype(BF)


def hand_on(*refs):
    count = len(refs) // 2
    for i in range(count):
        refs[count + i][...] = refs[i][...]


def shards(grad_parts, owner_of, stats_left, stats_right, basis_left, basis_right, moment_first, moment_second):
    blocks = owner_of.shape[0]
    padded = jnp.pad(owner_of[:, 0], (0, PADB - blocks), constant_values=-1)
    anywhere = pl.BlockSpec(memory_space=pl.ANY)
    vmem = pl.BlockSpec(memory_space=pltpu.VMEM)
    rows = (SLOTS, 32, 512)
    dma = pltpu.SemaphoreType.DMA
    scratch = [
        pltpu.VMEM((1152, 256), BF),
        pltpu.VMEM((1152, 256), BF),
        pltpu.VMEM((4, NB, 512), BF),
        pltpu.VMEM((2, 2, NB, 512), BF),
        pltpu.VMEM((2, 2, NB, 512), BF),
        pltpu.VMEM((2, NB, 512), BF),
        pltpu.VMEM((PADB, 512), BF),
        pltpu.VMEM((4, 640, PADB), BF),
        pltpu.VMEM((SLOTS, 8, 16, 128), BF),
        pltpu.VMEM((SLOTS, NZ, 16, 128), BF),
        pltpu.VMEM((SLOTS, NX, 4, 16, 128), BF),
        pltpu.VMEM((SLOTS, NY, 4, 64, 128), BF),
        pltpu.VMEM((SLOTS, 512, 512), BF),
        pltpu.VMEM((SLOTS, 4, 2, 64, 512), BF),
        pltpu.VMEM((3, 4, 2, 64, 512), BF),
        pltpu.VMEM(rows, BF),
        pltpu.VMEM(rows, BF),
        pltpu.VMEM(rows, F32),
        pltpu.VMEM(rows, F32),
        pltpu.VMEM(rows, BF),
        pltpu.VMEM(rows, BF),
        pltpu.VMEM(rows, F32),
        pltpu.VMEM(rows, F32),
        pltpu.VMEM((SLOTS, 512, 256), BF),
        pltpu.VMEM((SLOTS, 16, 32, 128), BF),
        pltpu.VMEM((SLOTS, NY, 32, 128), BF),
        pltpu.VMEM((512, 512), BF),
        pltpu.VMEM((512, 512), BF),
        pltpu.VMEM((256, 256), BF),
        pltpu.VMEM((512, 512), BF),
        pltpu.VMEM((256, 256), BF),
        pltpu.VMEM((512, PADB), BF),
        pltpu.VMEM((256, 512), BF),
        pltpu.VMEM((3, NY, 32, 128), BF),
        pltpu.VMEM((3, 16, 32, 128), BF),
        pltpu.VMEM((2, 512, 128), BF),
        pltpu.VMEM((NZ, 16, 128), BF),
        pltpu.VMEM((2, NZ, 32, 128), BF),
        pltpu.VMEM((NZ, 16, 128), BF),
        pltpu.VMEM((3, NX, 8, 16, 128), BF),
        pltpu.VMEM((4, NX, 8, 16, 128), BF),
        dma((8,)),
        dma((4,)),
        dma((1,)), dma((3,)),
        dma((1,)), dma((2, 2, SUBS)), dma((SUBS,)),
        dma((1,)), dma((1,)),
        dma((1,)), dma((SLOTS,)),
        dma((1,)), dma((SLOTS,)),
        dma((1,)), dma((SLOTS,)),
        dma((1,)), dma((SLOTS,)),
        dma((1,)), dma((2, 4, 2)),
        dma((1,)), dma((2,)),
        dma((3,)), dma((3,)),
        dma((3,)), dma((3,)),
        dma((3,)), dma((3,)),
        dma((2,)), dma((2,)),
    ]
    shapes = (
        jax.ShapeDtypeStruct(rows, BF),
        jax.ShapeDtypeStruct(rows, BF),
        jax.ShapeDtypeStruct(rows, F32),
        jax.ShapeDtypeStruct(rows, F32),
        jax.ShapeDtypeStruct((256, blocks), BF),
    )
    results = pl.pallas_call(
        kernel,
        out_shape=shapes,
        in_specs=[anywhere, vmem] + [anywhere] * 6,
        out_specs=(anywhere,) * 4 + (vmem,),
        scratch_shapes=scratch,
        compiler_params=pltpu.CompilerParams(
            collective_id=0, has_side_effects=True, vmem_limit_bytes=56 * 1024 * 1024
        ),
    )(
        grad_parts[0].reshape(blocks * 8, 512),
        padded[None, :],
        stats_left[0],
        stats_right[0],
        basis_left[0],
        basis_right[0].reshape(SLOTS, 4, 2, 64, 512),
        moment_first[0],
        moment_second[0],
    )
    new_left, new_right, new_first, new_second, picked = pl.pallas_call(
        hand_on,
        out_shape=shapes,
        in_specs=[vmem] * 5,
        out_specs=(vmem,) * 5,
    )(*results)
    update = picked.reshape(8, 32, blocks).transpose(2, 0, 1)
    return (new_left[None], new_right[None], new_first[None], new_second[None], update)


def solution(mesh):
    return jax.shard_map(
        shards,
        mesh=mesh,
        in_specs=(
            P("replica", None, "owner", None),
            P(),
            P("owner", None, "replica", None),
            P("owner", None, "replica", None),
            P("owner", None, None, None),
            P("owner", None, None, None),
            P("owner", None, "replica", None),
            P("owner", None, "replica", None),
        ),
        out_specs=(
            P("owner", None, "replica", None),
            P("owner", None, "replica", None),
            P("owner", None, "replica", None),
            P("owner", None, "replica", None),
            P(None, "owner", "replica"),
        ),
        check_vma=False,
    )
```

```python
import jax
import jax.numpy as jnp
from jax import lax
from jax.experimental import pallas as pl
from jax.experimental.pallas import tpu as pltpu
from jax.sharding import PartitionSpec as P

BETA_FIRST = 0.9
BETA_SECOND = 0.95
EPSILON = 1e-08
MESH = pl.DeviceIdType.MESH
BF = jnp.bfloat16
F32 = jnp.float32
NY, NX, NZ = 8, 4, 16
NB, PADB = 144, 256
SLOTS = 5
SUBS, SUBROWS = 3, 48
PAIRS = ((0, 1), (2, 3), (4, 4))
PAIR_CORE = (0, 1, 0)


def mm(a, b):
    return jnp.dot(a, b, preferred_element_type=F32)


def mm_t(a, b):
    return lax.dot_general(a, b, (((1,), (1,)), ((), ())), preferred_element_type=F32)


def iota(shape, axis):
    return lax.broadcasted_iota(jnp.int32, shape, axis)


def onehot(a, b):
    return jnp.where(a == b, 1.0, 0.0).astype(BF)


def kernel(
    grad, own_row, stats_l, stats_r, basis_l, basis_r, mom1, mom2,
    out_l, out_r, out_1, out_2, out_u,
    owners, go, gx, chunk, rs_mid, rs_end, rs_send, summed, place, v1, w1, xs1, gall,
    ql, qr, qrs, sl, sr, m1, m2, ol, orr, o1, o2, qlt, hsend, hrecv, gf, pm, perm2, perm3, perm4, oh2, wbuf,
    bmsg, bb, ub, ub4, w2, w24, xs2, yb,
    s_in, s_out, s_core, r_core, s_rs, r_mid, r_end, s_cag, r_cag, s_z1, r_z1, s_x1, r_x1,
    s_h, r_h, s_own, r_own, s_ag, r_ag, s_sib, r_sib, s_b, r_b, s_z2, r_z2, s_x2, r_x2, s_y, r_y,
):
    rep = lax.axis_index("replica")
    own = lax.axis_index("owner")
    y, c = rep // 2, rep % 2
    z, x = own // NX, own % NX
    sib = (y * 2 + (1 - c), own)
    zhalf = z // 8
    active = c == zhalf

    def at_y(yy, cc):
        return (lax.rem(yy + 2 * NY, NY) * 2 + cc, own)

    def at_z(zz):
        return (rep, zz * NX + x)

    def at_x(xx):
        return (rep, z * NX + xx)

    def remote(src, dst, ssem, rsem, dev):
        return pltpu.make_async_remote_copy(
            src_ref=src, dst_ref=dst, send_sem=ssem, recv_sem=rsem, device_id=dev, device_id_type=MESH
        )

    def received(ref, sem):
        remote(ref, ref, sem, sem, sib).wait_recv()

    def sent(ref, sem):
        remote(ref, ref, sem, sem, sib).wait_send()

    half = pl.ds(pl.multiple_of(c * 256, 256), 256)
    other = pl.ds(pl.multiple_of((1 - c) * 256, 256), 256)
    loads = [pltpu.make_async_copy(grad.at[:, half], go, s_in.at[0])]
    loads += [
        pltpu.make_async_copy(src, dst, s_in.at[1 + i])
        for i, (src, dst) in enumerate(
            ((basis_l, ql), (basis_r, qr), (stats_l, sl), (stats_r, sr), (mom1, m1), (mom2, m2))
        )
    ]
    swaps = [
        pltpu.make_async_copy(basis_r.at[k, :, h], qrs.at[i, :, 1 - h], s_in.at[7])
        for i, k in enumerate((1, 3, 4))
        for h in range(2)
    ]
    loads[0].start()
    drains = []

    barrier = pltpu.get_barrier_semaphore()
    for d in range(1, 16):
        pl.semaphore_signal(barrier, inc=1, device_id=(lax.rem(rep + d, 16), own), device_id_type=MESH)
    for d in range(1, NZ):
        pl.semaphore_signal(barrier, inc=1, device_id=at_z(lax.rem(z + d, NZ)), device_id_type=MESH)
    for d in range(1, NX):
        for cc in range(2):
            to = (y * 2 + cc, z * NX + lax.rem(x + d, NX))
            pl.semaphore_signal(barrier, inc=1, device_id=to, device_id_type=MESH)
    pl.semaphore_wait(barrier, 15 + NZ - 1 + 2 * (NX - 1))

    def core_copy(j):
        rows = pl.ds(j * 384, 384)
        return remote(grad.at[rows, other], gx.at[rows], s_core.at[0], r_core.at[j], sib)

    def rs_target(step):
        t = lax.rem(y + step + NY, NY)
        return (t // 4) * 2 + t % 2, c == (t % 4) // 2

    def rs_copy(d, step, j):
        sign = 1 - 2 * d
        rows = pl.ds(j * SUBROWS, SUBROWS)
        which = rs_target(sign * step)[0]
        if step == 4:
            lanes = pl.ds(d * 256, 256)
            src, dst = chunk.at[which, rows, lanes], rs_mid.at[d, 0, rows, lanes]
            sem, to = r_mid.at[d, 0, j], y + 2 * sign
        elif step == 3:
            src, dst = chunk.at[which, rows], rs_mid.at[d, 1, rows]
            sem, to = r_mid.at[d, 1, j], y + sign
        elif step == 2:
            src, dst = rs_send.at[d, rows], rs_end.at[d, 1, rows]
            sem, to = r_end.at[j], y + 2 * sign
        else:
            src, dst = chunk.at[which, rows], rs_end.at[d, 0, rows]
            sem, to = r_end.at[j], y + sign
        return remote(src, dst, s_rs.at[0], sem, at_y(to, c))

    def rs_start(step, j):
        for d in range(2):

            @pl.when(rs_target((1 - 2 * d) * step)[1])
            def _():
                rs_copy(d, step, j).start()

    for j in range(3):
        core_copy(j).start()
    for d in loads[1:] + swaps:
        d.start()

    out_of = iota((128, 1), 0)
    perm1 = onehot(iota((128, 128), 1), (out_of % 16) * 8 + out_of // 16)
    owners[...] = jnp.full((1, PADB), -1, jnp.int32)
    owners[:, pl.ds(0, NB)] = own_row[...]
    o_row = owners[...]
    e_row = onehot(iota((128, PADB), 0), o_row)
    before = mm(e_row, onehot_lt(iota((PADB, PADB), 0), iota((PADB, PADB), 1)))
    k_row = jnp.sum(before * e_row.astype(F32), axis=0, keepdims=True).astype(jnp.int32)
    zr, xr = o_row >> 2, o_row & 3
    code = jnp.where((zr >> 3) == c, (k_row * 8 + (zr & 7)) * 16 + xr, -64)
    for q in range(4):
        place[q] = onehot(iota((640, PADB), 0), code + 4 * q)
    side = jnp.where(k_row == 4, x >> 1, (k_row + y) & 1)
    slot_code = side * 256 + (k_row >> 1) * 64 + xr * 16 + zr
    summed[pl.ds(NB, PADB - NB), :] = jnp.zeros((PADB - NB, 512), BF)

    loads[0].wait()
    for j in range(3):
        core_copy(j).wait_recv()
        for g in range(3 * j, 3 * j + 3):
            rows = pl.ds(g * 128, 128)
            both = (mm(perm1, go[rows, :]) + mm(perm1, gx[rows, :])).astype(BF)
            for i in range(8):
                for q in range(2):
                    chunk[(i // 4) * 2 + q, pl.ds(g * 16, 16), pl.ds((i % 4) * 128, 128)] = both[
                        i * 16 : i * 16 + 16, q * 128 : q * 128 + 128
                    ]

        rs_start(4, j)
        rs_start(3, j)
    drains.append(lambda: sent(gx, s_core.at[0]))
    for j in range(SUBS):
        rs_start(1, j)

    for d in loads[1:]:
        d.wait()
    pltpu.make_async_copy(qrs, qrs, s_in.at[7]).wait()
    r_col = iota((256, 1), 0)
    held = ((r_col & 15) * 4 + ((r_col >> 4) & 3)) * 8 + (y // 4) * 4 + (r_col >> 6)
    held_rows = onehot(iota((256, 512), 1), held)
    same = onehot(iota((512, 512), 0), iota((512, 512), 1))

    def turn_basis(k):
        qlt[k] = mm_t(same, mm(held_rows, ql[k]).astype(BF)).astype(BF)

    turn_basis(0)
    turn_basis(1)
    turn_basis(2)

    for j in range(SUBS):
        for d in range(2):
            rows = pl.ds(j * SUBROWS, SUBROWS)
            t, here = rs_target((1 - 2 * d) * 2)

            @pl.when(here)
            def _():
                lanes = pl.ds(d * 256, 256)
                rest = pl.ds((1 - d) * 256, 256)
                received(rs_mid.at[d, 0, rows, lanes], r_mid.at[d, 0, j])
                received(rs_mid.at[d, 1, rows], r_mid.at[d, 1, j])
                rs_send[d, rows, lanes] = (
                    chunk[t, rows, lanes].astype(F32)
                    + rs_mid[d, 0, rows, lanes].astype(F32)
                    + rs_mid[d, 1, rows, lanes].astype(F32)
                ).astype(BF)
                rs_send[d, rows, rest] = (
                    chunk[t, rows, rest].astype(F32) + rs_mid[d, 1, rows, rest].astype(F32)
                ).astype(BF)
                rs_copy(d, 2, j).start()

    turn_basis(3)
    turn_basis(4)
    j2 = iota((256, 1), 0)
    perm2[...] = onehot(iota((256, 256), 1), (j2 & 15) * 16 + ((j2 >> 4) & 3) * 4 + (j2 >> 6))
    rho = iota((1, 512), 1)
    natural = ((rho & 15) * 4 + ((rho >> 4) & 3)) * 8 + (rho >> 8) * 4 + ((rho >> 6) & 3)
    pm[...] = onehot(iota((512, 512), 0), natural)
    last, sums_here = rs_target(0)
    sums = summed.at[pl.ds(0, NB)]

    @pl.when(sums_here)
    def _():
        for j in range(SUBS):
            rows = pl.ds(j * SUBROWS, SUBROWS)
            received(rs_end.at[:, :, rows], r_end.at[j])
            total = chunk[last, rows].astype(F32)
            for d in range(2):
                total += rs_end[d, 0, rows].astype(F32) + rs_end[d, 1, rows].astype(F32)
            summed[rows] = total.astype(BF)
            ref = summed.at[rows]
            remote(ref, ref, s_cag.at[0], r_cag.at[0], sib).start()

    @pl.when(jnp.logical_not(sums_here))
    def _():
        received(sums, r_cag.at[0])

    def drain_2():
        @pl.when(sums_here)
        def _():
            sent(chunk.at[pl.ds(0, 3)], s_rs.at[0])
            sent(sums, s_cag.at[0])

        @pl.when(jnp.logical_not(sums_here))
        def _():
            sent(chunk, s_rs.at[0])

    drains.append(drain_2)

    def z1_copy(k, j):
        low = lax.rem(z + j + 4 * active.astype(jnp.int32), 8)
        return remote(v1.at[k, low], w1.at[k, z], s_z1.at[0], r_z1.at[k], at_z(c * 8 + low))

    def fill_slots(k, n):
        rows = pl.ds(k * 128, n * 128)
        placed = mm(place[0, rows], summed[:, pl.ds(0, 128)])
        for q in range(1, 4):
            placed += mm(place[q, rows], summed[:, pl.ds(q * 128, 128)])
        v1[pl.ds(k, n)] = placed.astype(BF).reshape(n, 8, 16, 128)
        for kk in range(k, k + n):
            for j in (0, 1, 7, 2, 6, 3, 5):
                z1_copy(kk, j).start()

            @pl.when(jnp.logical_not(active))
            def _():
                z1_copy(kk, 4).start()

        @pl.when(active)
        def _():
            w1[pl.ds(k, n), z] = v1[pl.ds(k, n), lax.rem(z, 8)]

    fill_slots(0, 1)
    fill_slots(1, 4)

    def drain_3():
        @pl.when(jnp.logical_not(active))
        def _():
            sent(v1, s_z1.at[0])

        @pl.when(active)
        def _():
            sent(v1.at[:, pl.ds(0, 7)], s_z1.at[0])
            sent(xs1.at[:, pl.ds(0, NX - 1)], s_x1.at[0])

    drains.append(drain_3)

    mine = onehot(iota((32, 512), 1), iota((32, 512), 0) + rep * 32)

    def x1_copy(k, j):
        to = lax.rem(x + j, NX)
        rows = pl.ds(pl.multiple_of(x * 16, 16), 16)
        return remote(xs1.at[k, to], gall.at[k, y, :, rows], s_x1.at[0], r_x1.at[k], at_x(to))

    def regroup_slot(k):
        received(w1.at[k, pl.ds(0, NZ - 1)], r_z1.at[k])
        xs1[k] = mm(perm2[...], w1[k].reshape(256, 128)).astype(BF).reshape(NX, 4, 16, 128)
        for j in (2, 1, 3):
            x1_copy(k, j).start()
        gall[k, y, :, pl.ds(pl.multiple_of(x * 16, 16), 16)] = xs1[k, x]

    def h_copy(k, dy, cc):
        to = lax.rem(y + dy, NY) * 2 + cc
        return remote(hsend.at[k, to], hrecv.at[k, y], s_h.at[0], r_h.at[k], (to, own))

    def own_copy(k):
        ref = gall.at[k, y]
        return remote(ref, ref, s_own.at[0], r_own.at[k], sib)

    far_first = (4, 3, 5, 2, 6, 1, 7)

    def left_product(k):
        received(xs1.at[k, pl.ds(0, NX - 1)], r_x1.at[k])
        hsend[k] = mm(qlt[k], gall[k, y].reshape(256, 128)).astype(BF).reshape(16, 32, 128)
        for dy in far_first:
            for cc in range(2):
                h_copy(k, dy, cc).start()
        for cc in range(2):

            @pl.when(c != cc)
            def _():
                h_copy(k, 0, cc).start()

        hrecv[k, y] = hsend[k, rep]
        own_copy(k).start()

    def ag_part(k, t, s, d):
        return gall.at[k, t] if s < 3 else gall.at[k, t, pl.ds(d * 2, 2)]

    def ag_copy(d, s, k):
        sign = 1 - 2 * d
        ref = ag_part(k, lax.rem(y - sign * s + NY, NY), s, d)
        return remote(ref, ref, s_ag.at[0], r_ag.at[d, s, k], at_y(y + sign, c))

    def ag_arrival(d, s, k):
        return ag_part(k, lax.rem(y - (1 - 2 * d) * (s + 1) + NY, NY), s, d)

    def gather(s, ks):
        @pl.when(jnp.logical_not(active))
        def _():
            for k in ks:
                if s == 0:
                    received(gall.at[k, y], r_own.at[k])
                for d in range(2):
                    if s > 0:
                        received(ag_arrival(d, s - 1, k), r_ag.at[d, s - 1, k])
                    if s < 4:
                        ag_copy(d, s, k).start()
                if s > 0:
                    for d in range(2):
                        ref = ag_arrival(d, s - 1, k)
                        remote(ref, ref, s_sib.at[0], r_sib.at[k], sib).start()

    @pl.when(active)
    def _():
        regroup_slot(0)
        regroup_slot(1)
        for k in range(SLOTS):
            if k + 2 < SLOTS:
                regroup_slot(k + 2)
            left_product(k)

    def out_copies(k):
        return [
            pltpu.make_async_copy(src.at[k], dst.at[k], s_out.at[i])
            for i, (src, dst) in enumerate(((o1, out_1), (o2, out_2), (ol, out_l), (orr, out_r)))
        ]

    lane_low = iota((32, 128), 1) < 64
    back = {}

    def slot_products(k):
        @pl.when(active)
        def _():
            received(hrecv.at[k, pl.ds(0, NY - 1)], r_h.at[k])

        @pl.when(jnp.logical_not(active))
        def _():
            received(hrecv.at[k], r_h.at[k])

        h = jnp.concatenate(
            [(hrecv[k, q].astype(F32) + hrecv[k, q + 4].astype(F32)).astype(BF) for q in range(4)], axis=1
        )
        rotated = mm(h, qr[k].reshape(512, 512))
        first = BETA_FIRST * m1[k] + (1.0 - BETA_FIRST) * rotated
        second = BETA_SECOND * m2[k] + (1.0 - BETA_SECOND) * rotated * rotated
        o1[k] = first
        o2[k] = second
        for copy in out_copies(k)[:2]:
            copy.start()
        direction = (first / (jnp.sqrt(second) + EPSILON)).astype(BF)
        if k in (0, 2, 4):
            back[k, 0] = mm_t(direction, qr[k].reshape(512, 512)).astype(BF)
        if k in (1, 3, 4):
            back[k, 1] = mm_t(direction, qrs[(k - 1) // 2 if k < 4 else 2].reshape(512, 512)).astype(BF)

    def b_copy(p, dy):
        yy = lax.rem(y + dy, NY)
        return remote(bmsg.at[p, yy], bb.at[p, rep], s_b.at[p], r_b.at[p], (yy * 2 + PAIR_CORE[p], own))

    def send_back(p):
        a, b = PAIRS[p]
        for yy in range(NY):
            lanes = slice((yy // 2) * 128, (yy // 2) * 128 + 128)
            lo, hi = back[a, 0][:, lanes], back[b, 1][:, lanes]
            bmsg[p, yy] = jnp.where(lane_low, lo, hi) if yy % 2 == 0 else jnp.where(lane_low, hi, lo)
        for dy in far_first:
            b_copy(p, dy).start()

        @pl.when(c != PAIR_CORE[p])
        def _():
            b_copy(p, 0).start()

        @pl.when(c == PAIR_CORE[p])
        def _():
            bb[p, rep] = bmsg[p, y]

    def stat_products(k):
        @pl.when(active)
        def _():
            received(gall.at[k, pl.ds(0, NY - 1)], r_sib.at[k])

        for t in range(NY):
            gf[pl.ds((t // 4) * 256, 256), pl.ds((t % 4) * 128, 128)] = gall[k, t].reshape(256, 128)
        columns = mm_t(mine, gf[...]).astype(BF)
        right = mm(columns, gf[...])
        orr[k] = (BETA_SECOND * sr[k].astype(F32) + (1.0 - BETA_SECOND) * right).astype(BF)
        rows = mm(pm[pl.ds(pl.multiple_of(rep * 32, 32), 32), :], gf[...]).astype(BF)
        left = mm_t(mm_t(rows, gf[...]).astype(BF), pm[...])
        ol[k] = (BETA_SECOND * sl[k].astype(F32) + (1.0 - BETA_SECOND) * left).astype(BF)
        for copy in out_copies(k)[2:]:
            copy.start()

    def z2_copy(p, j):
        to = lax.rem(z + j, NZ)
        if p == 2:
            src, dst = ub4.at[to], w24.at[z]
        else:
            src, dst = ub.at[p, pl.ds(pl.multiple_of(to * 32, 32), 32)], w2.at[p, z]
        return remote(src, dst, s_z2.at[p], r_z2.at[p], at_z(to))

    def x2_copy(p, j, cc):
        to = lax.rem(x + j, NX)
        part = lax.rem(to, 2) if p == 2 else to
        return remote(xs2.at[p, part], yb.at[p, x], s_x2.at[p], r_x2.at[p], (y * 2 + cc, z * NX + to))

    def y_copy(p):
        return remote(yb.at[p], yb.at[p], s_y.at[p], r_y.at[p], sib)

    def update_products(p):
        received(bb.at[p, pl.ds(0, 15)], r_b.at[p])
        a, b = PAIRS[p]
        columns = bb[p].reshape(512, 128)
        if p == 2:
            whole = mm(ql[a], columns).astype(BF).reshape(NZ, 2, 16, 128)
            low = iota((NZ, 16, 128), 2) < 64
            ub4[...] = jnp.where(low, whole[:, 0], whole[:, 1])
        else:
            swap = jnp.where(iota((512, 128), 1) < 64, 0, 1) == (y & 1)
            ub[p] = jnp.where(swap, mm(ql[a], columns), mm(ql[b], columns)).astype(BF)
        for j in (8, 7, 9, 6, 10, 5, 11, 4, 12, 3, 13, 2, 14, 1, 15):
            z2_copy(p, j).start()
        if p == 2:
            w24[z] = ub4[z]
        else:
            w2[p, z] = ub[p, pl.ds(pl.multiple_of(z * 32, 32), 32)]

    def update_regroup(p):
        if p == 2:
            received(w24.at[pl.ds(0, NZ - 1)], r_z2.at[p])
            parts = mm(perm4[...], w24[...].reshape(256, 128)).astype(BF).reshape(2, 8, 16, 128)
            xs2[p, pl.ds(0, 2)] = parts
            for j in (2, 1, 3, 0):
                for cc in (1, 0)[: 1 + (j > 0)]:
                    x2_copy(p, j, cc).start()
            yb[p, x] = xs2[p, lax.rem(x, 2)]
        else:
            received(w2.at[p, pl.ds(0, NZ - 1)], r_z2.at[p])
            xs2[p] = mm(perm3[...], w2[p].reshape(512, 128)).astype(BF).reshape(NX, 8, 16, 128)
            for j in (2, 1, 3):
                x2_copy(p, j, PAIR_CORE[p]).start()
            yb[p, x] = xs2[p, x]

    def update_share(p):
        received(yb.at[p, pl.ds(0, NX - 1)], r_x2.at[p])
        if p != 2:
            y_copy(p).start()

    def on_core(core, step, p):
        @pl.when(c == core)
        def _():
            step(p)

    slot_products(0)
    gather(0, (0, 1, 2))
    slot_products(1)
    send_back(0)
    gather(0, (3, 4))
    slot_products(2)
    slot_products(3)
    send_back(1)
    gather(1, (0, 1))
    slot_products(4)
    send_back(2)
    gather(1, (2, 3, 4))
    j3 = iota((512, 1), 0)
    perm3[...] = onehot(iota((512, 512), 1), (j3 & 15) * 32 + (j3 >> 7) * 8 + ((j3 >> 4) & 7))
    perm4[...] = onehot(iota((256, 256), 1), (j2 & 15) * 16 + (j2 >> 7) * 8 + ((j2 >> 4) & 7))
    oh2[...] = onehot(iota((512, PADB), 0), slot_code)
    yb[pl.ds(3, 1)] = jnp.zeros((1, NX, 8, 16, 128), BF)
    on_core(0, update_products, 0)
    gather(2, (0, 1))
    on_core(1, update_products, 1)
    gather(2, (2,))
    on_core(0, update_products, 2)
    gather(2, (3, 4))
    gather(3, (0, 1, 2))
    on_core(0, update_regroup, 0)
    gather(3, (3, 4))
    gather(4, (0, 1))
    stat_products(0)
    gather(4, (2,))
    on_core(1, update_regroup, 1)
    gather(4, (3, 4))
    stat_products(1)
    on_core(0, update_share, 0)
    on_core(0, update_regroup, 2)
    stat_products(2)
    on_core(1, update_share, 1)
    stat_products(3)
    stat_products(4)

    @pl.when(c == 0)
    def _():
        update_share(2)
        received(yb.at[1], r_y.at[1])

    @pl.when(c == 1)
    def _():
        received(yb.at[0], r_y.at[0])
        received(yb.at[2], r_x2.at[2])

    chosen = onehot(
        iota((64, 128), 1), (iota((64, 1), 0) >> 5) * 64 + 32 * c + (iota((64, 1), 0) & 31)
    )
    for i in range(8):
        lanes = mm_t(chosen, yb[:, :, i].reshape(256, 128)).astype(BF)
        wbuf[pl.ds(i * 32, 32), pl.ds(0, 256)] = lanes[:32]
        wbuf[pl.ds(i * 32, 32), pl.ds(256, 256)] = lanes[32:]
    out_u[...] = mm(wbuf[...], oh2[...]).astype(BF)[:, :NB]

    def drain_4():
        @pl.when(active)
        def _():
            sent(hsend.at[:, pl.ds(0, 15)], s_h.at[0])
            sent(gall.at[:, 0], s_own.at[0])

        @pl.when(jnp.logical_not(active))
        def _():
            sent(gall.at[:, pl.ds(0, 7)], s_ag.at[0])
            sent(gall.at[:, pl.ds(0, 7)], s_sib.at[0])

        for p in range(3):

            @pl.when(c != PAIR_CORE[p])
            def _():
                sent(bmsg.at[p], s_b.at[p])

            @pl.when(c == PAIR_CORE[p])
            def _():
                sent(bmsg.at[p, pl.ds(0, 7)], s_b.at[p])
                if p == 2:
                    sent(ub4.at[pl.ds(0, NZ - 1)], s_z2.at[p])
                    sent(gall.at[0, pl.ds(0, 7), pl.ds(0, 2)], s_x2.at[p])
                else:
                    sent(w2.at[p, pl.ds(0, NZ - 1)], s_z2.at[p])
                    sent(yb.at[p, pl.ds(0, NX - 1)], s_x2.at[p])
                    sent(yb.at[p], s_y.at[p])

    drains.append(drain_4)
    for i, (src, dst) in enumerate(((o1, out_1), (o2, out_2), (ol, out_l), (orr, out_r))):
        pltpu.make_async_copy(src, dst, s_out.at[i]).wait()
    for drain in drains:
        drain()


def onehot_lt(a, b):
    return jnp.where(a < b, 1.0, 0.0).astype(BF)


def hand_on(*refs):
    count = len(refs) // 2
    for i in range(count):
        refs[count + i][...] = refs[i][...]


def shards(grad_parts, owner_of, stats_left, stats_right, basis_left, basis_right, moment_first, moment_second):
    blocks = owner_of.shape[0]
    anywhere = pl.BlockSpec(memory_space=pl.ANY)
    vmem = pl.BlockSpec(memory_space=pltpu.VMEM)
    rows = (SLOTS, 32, 512)
    dma = pltpu.SemaphoreType.DMA
    scratch = [
        pltpu.VMEM((1, PADB), jnp.int32),
        pltpu.VMEM((1152, 256), BF),
        pltpu.VMEM((1152, 256), BF),
        pltpu.VMEM((4, NB, 512), BF),
        pltpu.VMEM((2, 2, NB, 512), BF),
        pltpu.VMEM((2, 2, NB, 512), BF),
        pltpu.VMEM((2, NB, 512), BF),
        pltpu.VMEM((PADB, 512), BF),
        pltpu.VMEM((4, 640, PADB), BF),
        pltpu.VMEM((SLOTS, 8, 16, 128), BF),
        pltpu.VMEM((SLOTS, NZ, 16, 128), BF),
        pltpu.VMEM((SLOTS, NX, 4, 16, 128), BF),
        pltpu.VMEM((SLOTS, NY, 4, 64, 128), BF),
        pltpu.VMEM((SLOTS, 512, 512), BF),
        pltpu.VMEM((SLOTS, 4, 2, 64, 512), BF),
        pltpu.VMEM((3, 4, 2, 64, 512), BF),
        pltpu.VMEM(rows, BF),
        pltpu.VMEM(rows, BF),
        pltpu.VMEM(rows, F32),
        pltpu.VMEM(rows, F32),
        pltpu.VMEM(rows, BF),
        pltpu.VMEM(rows, BF),
        pltpu.VMEM(rows, F32),
        pltpu.VMEM(rows, F32),
        pltpu.VMEM((SLOTS, 512, 256), BF),
        pltpu.VMEM((SLOTS, 16, 32, 128), BF),
        pltpu.VMEM((SLOTS, NY, 32, 128), BF),
        pltpu.VMEM((512, 512), BF),
        pltpu.VMEM((512, 512), BF),
        pltpu.VMEM((256, 256), BF),
        pltpu.VMEM((512, 512), BF),
        pltpu.VMEM((256, 256), BF),
        pltpu.VMEM((512, PADB), BF),
        pltpu.VMEM((256, 512), BF),
        pltpu.VMEM((3, NY, 32, 128), BF),
        pltpu.VMEM((3, 16, 32, 128), BF),
        pltpu.VMEM((2, 512, 128), BF),
        pltpu.VMEM((NZ, 16, 128), BF),
        pltpu.VMEM((2, NZ, 32, 128), BF),
        pltpu.VMEM((NZ, 16, 128), BF),
        pltpu.VMEM((3, NX, 8, 16, 128), BF),
        pltpu.VMEM((4, NX, 8, 16, 128), BF),
        dma((8,)),
        dma((4,)),
        dma((1,)), dma((3,)),
        dma((1,)), dma((2, 2, SUBS)), dma((SUBS,)),
        dma((1,)), dma((1,)),
        dma((1,)), dma((SLOTS,)),
        dma((1,)), dma((SLOTS,)),
        dma((1,)), dma((SLOTS,)),
        dma((1,)), dma((SLOTS,)),
        dma((1,)), dma((2, 4, SLOTS)),
        dma((1,)), dma((SLOTS,)),
        dma((3,)), dma((3,)),
        dma((3,)), dma((3,)),
        dma((3,)), dma((3,)),
        dma((2,)), dma((2,)),
    ]
    shapes = (
        jax.ShapeDtypeStruct(rows, BF),
        jax.ShapeDtypeStruct(rows, BF),
        jax.ShapeDtypeStruct(rows, F32),
        jax.ShapeDtypeStruct(rows, F32),
        jax.ShapeDtypeStruct((256, blocks), BF),
    )
    results = pl.pallas_call(
        kernel,
        out_shape=shapes,
        in_specs=[anywhere, vmem] + [anywhere] * 6,
        out_specs=(anywhere,) * 4 + (vmem,),
        scratch_shapes=scratch,
        compiler_params=pltpu.CompilerParams(
            collective_id=0, has_side_effects=True, vmem_limit_bytes=56 * 1024 * 1024
        ),
    )(
        grad_parts[0].reshape(blocks * 8, 512),
        owner_of.reshape(1, blocks),
        stats_left[0],
        stats_right[0],
        basis_left[0],
        basis_right[0].reshape(SLOTS, 4, 2, 64, 512),
        moment_first[0],
        moment_second[0],
    )
    new_left, new_right, new_first, new_second, picked = pl.pallas_call(
        hand_on,
        out_shape=shapes,
        in_specs=[vmem] * 5,
        out_specs=(vmem,) * 5,
    )(*results)
    update = picked.reshape(8, 32, blocks).transpose(2, 0, 1)
    return (new_left[None], new_right[None], new_first[None], new_second[None], update)


def solution(mesh):
    return jax.shard_map(
        shards,
        mesh=mesh,
        in_specs=(
            P("replica", None, "owner", None),
            P(),
            P("owner", None, "replica", None),
            P("owner", None, "replica", None),
            P("owner", None, None, None),
            P("owner", None, None, None),
            P("owner", None, "replica", None),
            P("owner", None, "replica", None),
        ),
        out_specs=(
            P("owner", None, "replica", None),
            P("owner", None, "replica", None),
            P("owner", None, "replica", None),
            P("owner", None, "replica", None),
            P(None, "owner", "replica"),
        ),
        check_vma=False,
    )
```

```python
import jax
import jax.numpy as jnp
from jax import lax
from jax.experimental import pallas as pl
from jax.experimental.pallas import tpu as pltpu
from jax.sharding import PartitionSpec as P

BETA_FIRST = 0.9
BETA_SECOND = 0.95
EPSILON = 1e-08
MESH = pl.DeviceIdType.MESH
BF = jnp.bfloat16
F32 = jnp.float32
NY, NX, NZ = 8, 4, 16
NB, PADB = 144, 256
SLOTS = 5
SUBS, SUBROWS = 3, 48
PAIRS = ((0, 1), (2, 3), (4, 4))
PAIR_CORE = (0, 1, 0)


def mm(a, b):
    return jnp.dot(a, b, preferred_element_type=F32)


def mm_t(a, b):
    return lax.dot_general(a, b, (((1,), (1,)), ((), ())), preferred_element_type=F32)


def iota(shape, axis):
    return lax.broadcasted_iota(jnp.int32, shape, axis)


def onehot(a, b):
    return jnp.where(a == b, 1.0, 0.0).astype(BF)


def kernel(
    grad, own_row, stats_l, stats_r, basis_l, basis_r, mom1, mom2,
    out_l, out_r, out_1, out_2, out_u,
    owners, go, gx, chunk, rs_mid, rs_end, rs_send, summed, place, v1, w1, xs1, gall,
    ql, qr, qrs, sl, sr, m1, m2, ol, orr, o1, o2, qlt, hsend, hrecv, gf, pm, perm2, perm3, perm4, oh2, wbuf,
    bmsg, bb, ub, ub4, w2, w24, xs2, yb,
    s_in, s_out, s_core, r_core, s_rs, r_mid, r_end, s_cag, r_cag, s_z1, r_z1, s_x1, r_x1,
    s_h, r_h, s_own, r_own, s_ag, r_ag, s_sib, r_sib, s_b, r_b, s_z2, r_z2, s_x2, r_x2, s_y, r_y,
):
    rep = lax.axis_index("replica")
    own = lax.axis_index("owner")
    y, c = rep // 2, rep % 2
    z, x = own // NX, own % NX
    sib = (y * 2 + (1 - c), own)
    zhalf = z // 8
    active = c == zhalf

    def at_y(yy, cc):
        return (lax.rem(yy + 2 * NY, NY) * 2 + cc, own)

    def at_z(zz):
        return (rep, zz * NX + x)

    def at_x(xx):
        return (rep, z * NX + xx)

    def remote(src, dst, ssem, rsem, dev):
        return pltpu.make_async_remote_copy(
            src_ref=src, dst_ref=dst, send_sem=ssem, recv_sem=rsem, device_id=dev, device_id_type=MESH
        )

    def received(ref, sem):
        remote(ref, ref, sem, sem, sib).wait_recv()

    def sent(ref, sem):
        remote(ref, ref, sem, sem, sib).wait_send()

    half = pl.ds(pl.multiple_of(c * 256, 256), 256)
    other = pl.ds(pl.multiple_of((1 - c) * 256, 256), 256)
    loads = [pltpu.make_async_copy(grad.at[:, half], go, s_in.at[0])]
    loads += [
        pltpu.make_async_copy(src, dst, s_in.at[1 + i])
        for i, (src, dst) in enumerate(
            ((basis_l, ql), (basis_r, qr), (stats_l, sl), (stats_r, sr), (mom1, m1), (mom2, m2))
        )
    ]
    swaps = [
        pltpu.make_async_copy(basis_r.at[k, :, h], qrs.at[i, :, 1 - h], s_in.at[7])
        for i, k in enumerate((1, 3, 4))
        for h in range(2)
    ]
    loads[0].start()
    drains = []

    barrier = pltpu.get_barrier_semaphore()
    for d in range(1, 16):
        pl.semaphore_signal(barrier, inc=1, device_id=(lax.rem(rep + d, 16), own), device_id_type=MESH)
    for d in range(1, NZ):
        pl.semaphore_signal(barrier, inc=1, device_id=at_z(lax.rem(z + d, NZ)), device_id_type=MESH)
    for d in range(1, NX):
        for cc in range(2):
            to = (y * 2 + cc, z * NX + lax.rem(x + d, NX))
            pl.semaphore_signal(barrier, inc=1, device_id=to, device_id_type=MESH)
    pl.semaphore_wait(barrier, 15 + NZ - 1 + 2 * (NX - 1))

    def core_copy(j):
        rows = pl.ds(j * 384, 384)
        return remote(grad.at[rows, other], gx.at[rows], s_core.at[0], r_core.at[j], sib)

    def rs_target(step):
        t = lax.rem(y + step + NY, NY)
        return (t // 4) * 2 + t % 2, c == (t % 4) // 2

    def rs_copy(d, step, j):
        sign = 1 - 2 * d
        rows = pl.ds(j * SUBROWS, SUBROWS)
        which = rs_target(sign * step)[0]
        if step == 4:
            lanes = pl.ds(d * 256, 256)
            src, dst = chunk.at[which, rows, lanes], rs_mid.at[d, 0, rows, lanes]
            sem, to = r_mid.at[d, 0, j], y + 2 * sign
        elif step == 3:
            src, dst = chunk.at[which, rows], rs_mid.at[d, 1, rows]
            sem, to = r_mid.at[d, 1, j], y + sign
        elif step == 2:
            src, dst = rs_send.at[d, rows], rs_end.at[d, 1, rows]
            sem, to = r_end.at[j], y + 2 * sign
        else:
            src, dst = chunk.at[which, rows], rs_end.at[d, 0, rows]
            sem, to = r_end.at[j], y + sign
        return remote(src, dst, s_rs.at[0], sem, at_y(to, c))

    def rs_start(step, j):
        for d in range(2):

            @pl.when(rs_target((1 - 2 * d) * step)[1])
            def _():
                rs_copy(d, step, j).start()

    for j in range(3):
        core_copy(j).start()
    for d in loads[1:] + swaps:
        d.start()

    out_of = iota((128, 1), 0)
    perm1 = onehot(iota((128, 128), 1), (out_of % 16) * 8 + out_of // 16)
    owners[...] = jnp.full((1, PADB), -1, jnp.int32)
    owners[:, pl.ds(0, NB)] = own_row[...]
    o_row = owners[...]
    e_row = onehot(iota((128, PADB), 0), o_row)
    before = mm(e_row, onehot_lt(iota((PADB, PADB), 0), iota((PADB, PADB), 1)))
    k_row = jnp.sum(before * e_row.astype(F32), axis=0, keepdims=True).astype(jnp.int32)
    zr, xr = o_row >> 2, o_row & 3
    code = jnp.where((zr >> 3) == c, (k_row * 8 + (zr & 7)) * 16 + xr, -64)
    for q in range(4):
        place[q] = onehot(iota((640, PADB), 0), code + 4 * q)
    side = jnp.where(k_row == 4, x >> 1, (k_row + y) & 1)
    slot_code = side * 256 + (k_row >> 1) * 64 + xr * 16 + zr
    summed[pl.ds(NB, PADB - NB), :] = jnp.zeros((PADB - NB, 512), BF)

    loads[0].wait()
    for j in range(3):
        core_copy(j).wait_recv()
        for g in range(3 * j, 3 * j + 3):
            rows = pl.ds(g * 128, 128)
            both = (mm(perm1, go[rows, :]) + mm(perm1, gx[rows, :])).astype(BF)
            for i in range(8):
                for q in range(2):
                    chunk[(i // 4) * 2 + q, pl.ds(g * 16, 16), pl.ds((i % 4) * 128, 128)] = both[
                        i * 16 : i * 16 + 16, q * 128 : q * 128 + 128
                    ]

        rs_start(4, j)
        rs_start(3, j)
    drains.append(lambda: sent(gx, s_core.at[0]))
    for j in range(SUBS):
        rs_start(1, j)

    for d in loads[1:]:
        d.wait()
    pltpu.make_async_copy(qrs, qrs, s_in.at[7]).wait()
    r_col = iota((256, 1), 0)
    held = ((r_col & 15) * 4 + ((r_col >> 4) & 3)) * 8 + (y // 4) * 4 + (r_col >> 6)
    held_rows = onehot(iota((256, 512), 1), held)
    same = onehot(iota((512, 512), 0), iota((512, 512), 1))

    def turn_basis(k):
        qlt[k] = mm_t(same, mm(held_rows, ql[k]).astype(BF)).astype(BF)

    turn_basis(0)
    turn_basis(1)
    turn_basis(2)

    for j in range(SUBS):
        for d in range(2):
            rows = pl.ds(j * SUBROWS, SUBROWS)
            t, here = rs_target((1 - 2 * d) * 2)

            @pl.when(here)
            def _():
                lanes = pl.ds(d * 256, 256)
                rest = pl.ds((1 - d) * 256, 256)
                received(rs_mid.at[d, 0, rows, lanes], r_mid.at[d, 0, j])
                received(rs_mid.at[d, 1, rows], r_mid.at[d, 1, j])
                rs_send[d, rows, lanes] = (
                    chunk[t, rows, lanes].astype(F32)
                    + rs_mid[d, 0, rows, lanes].astype(F32)
                    + rs_mid[d, 1, rows, lanes].astype(F32)
                ).astype(BF)
                rs_send[d, rows, rest] = (
                    chunk[t, rows, rest].astype(F32) + rs_mid[d, 1, rows, rest].astype(F32)
                ).astype(BF)
                rs_copy(d, 2, j).start()

    turn_basis(3)
    turn_basis(4)
    j2 = iota((256, 1), 0)
    perm2[...] = onehot(iota((256, 256), 1), (j2 & 15) * 16 + ((j2 >> 4) & 3) * 4 + (j2 >> 6))
    rho = iota((1, 512), 1)
    natural = ((rho & 15) * 4 + ((rho >> 4) & 3)) * 8 + (rho >> 8) * 4 + ((rho >> 6) & 3)
    pm[...] = onehot(iota((512, 512), 0), natural)
    last, sums_here = rs_target(0)
    sums = summed.at[pl.ds(0, NB)]

    @pl.when(sums_here)
    def _():
        for j in range(SUBS):
            rows = pl.ds(j * SUBROWS, SUBROWS)
            received(rs_end.at[:, :, rows], r_end.at[j])
            total = chunk[last, rows].astype(F32)
            for d in range(2):
                total += rs_end[d, 0, rows].astype(F32) + rs_end[d, 1, rows].astype(F32)
            summed[rows] = total.astype(BF)
            ref = summed.at[rows]
            remote(ref, ref, s_cag.at[0], r_cag.at[0], sib).start()

    @pl.when(jnp.logical_not(sums_here))
    def _():
        received(sums, r_cag.at[0])

    def drain_2():
        @pl.when(sums_here)
        def _():
            sent(chunk.at[pl.ds(0, 3)], s_rs.at[0])
            sent(sums, s_cag.at[0])

        @pl.when(jnp.logical_not(sums_here))
        def _():
            sent(chunk, s_rs.at[0])

    drains.append(drain_2)

    def z1_copy(k, j):
        low = lax.rem(z + j + 4 * active.astype(jnp.int32), 8)
        return remote(v1.at[k, low], w1.at[k, z], s_z1.at[0], r_z1.at[k], at_z(c * 8 + low))

    def fill_slots(k, n):
        rows = pl.ds(k * 128, n * 128)
        placed = mm(place[0, rows], summed[:, pl.ds(0, 128)])
        for q in range(1, 4):
            placed += mm(place[q, rows], summed[:, pl.ds(q * 128, 128)])
        v1[pl.ds(k, n)] = placed.astype(BF).reshape(n, 8, 16, 128)
        for kk in range(k, k + n):
            for j in (0, 1, 7, 2, 6, 3, 5):
                z1_copy(kk, j).start()

            @pl.when(jnp.logical_not(active))
            def _():
                z1_copy(kk, 4).start()

        @pl.when(active)
        def _():
            w1[pl.ds(k, n), z] = v1[pl.ds(k, n), lax.rem(z, 8)]

    fill_slots(0, 1)
    fill_slots(1, 4)

    def drain_3():
        @pl.when(jnp.logical_not(active))
        def _():
            sent(v1, s_z1.at[0])

        @pl.when(active)
        def _():
            sent(v1.at[:, pl.ds(0, 7)], s_z1.at[0])
            sent(xs1.at[:, pl.ds(0, NX - 1)], s_x1.at[0])

    drains.append(drain_3)

    mine = onehot(iota((32, 512), 1), iota((32, 512), 0) + rep * 32)

    def x1_copy(k, j):
        to = lax.rem(x + j, NX)
        rows = pl.ds(pl.multiple_of(x * 16, 16), 16)
        return remote(xs1.at[k, to], gall.at[k, y, :, rows], s_x1.at[0], r_x1.at[k], at_x(to))

    def regroup_slot(k):
        received(w1.at[k, pl.ds(0, NZ - 1)], r_z1.at[k])
        xs1[k] = mm(perm2[...], w1[k].reshape(256, 128)).astype(BF).reshape(NX, 4, 16, 128)
        for j in (2, 1, 3):
            x1_copy(k, j).start()
        gall[k, y, :, pl.ds(pl.multiple_of(x * 16, 16), 16)] = xs1[k, x]

    def h_copy(k, dy, cc):
        to = lax.rem(y + dy, NY) * 2 + cc
        return remote(hsend.at[k, to], hrecv.at[k, y], s_h.at[0], r_h.at[k], (to, own))

    def own_copy(k):
        ref = gall.at[k, y]
        return remote(ref, ref, s_own.at[0], r_own.at[k], sib)

    far_first = (4, 3, 5, 2, 6, 1, 7)

    def left_product(k):
        received(xs1.at[k, pl.ds(0, NX - 1)], r_x1.at[k])
        hsend[k] = mm(qlt[k], gall[k, y].reshape(256, 128)).astype(BF).reshape(16, 32, 128)
        for dy in far_first:
            for cc in range(2):
                h_copy(k, dy, cc).start()
        for cc in range(2):

            @pl.when(c != cc)
            def _():
                h_copy(k, 0, cc).start()

        hrecv[k, y] = hsend[k, rep]
        own_copy(k).start()

    def ag_part(k, t, s, d):
        return gall.at[k, t] if s < 3 else gall.at[k, t, pl.ds(d * 2, 2)]

    def ag_copy(d, s, k):
        sign = 1 - 2 * d
        ref = ag_part(k, lax.rem(y - sign * s + NY, NY), s, d)
        return remote(ref, ref, s_ag.at[0], r_ag.at[d, s, k], at_y(y + sign, c))

    def ag_arrival(d, s, k):
        return ag_part(k, lax.rem(y - (1 - 2 * d) * (s + 1) + NY, NY), s, d)

    def gather(s, ks):
        @pl.when(jnp.logical_not(active))
        def _():
            for k in ks:
                if s == 0:
                    received(gall.at[k, y], r_own.at[k])
                for d in range(2):
                    if s > 0:
                        received(ag_arrival(d, s - 1, k), r_ag.at[d, s - 1, k])
                    if s < 4:
                        ag_copy(d, s, k).start()
                if s > 0:
                    for d in range(2):
                        ref = ag_arrival(d, s - 1, k)
                        remote(ref, ref, s_sib.at[0], r_sib.at[k], sib).start()

    @pl.when(active)
    def _():
        regroup_slot(0)
        regroup_slot(1)
        for k in range(SLOTS):
            if k + 2 < SLOTS:
                regroup_slot(k + 2)
            left_product(k)

    def out_copies(k):
        return [
            pltpu.make_async_copy(src.at[k], dst.at[k], s_out.at[i])
            for i, (src, dst) in enumerate(((o1, out_1), (o2, out_2), (ol, out_l), (orr, out_r)))
        ]

    lane_low = iota((32, 128), 1) < 64
    back = {}

    def slot_products(k):
        @pl.when(active)
        def _():
            received(hrecv.at[k, pl.ds(0, NY - 1)], r_h.at[k])

        @pl.when(jnp.logical_not(active))
        def _():
            received(hrecv.at[k], r_h.at[k])

        h = jnp.concatenate(
            [(hrecv[k, q].astype(F32) + hrecv[k, q + 4].astype(F32)).astype(BF) for q in range(4)], axis=1
        )
        rotated = mm(h, qr[k].reshape(512, 512))
        first = BETA_FIRST * m1[k] + (1.0 - BETA_FIRST) * rotated
        second = BETA_SECOND * m2[k] + (1.0 - BETA_SECOND) * rotated * rotated
        o1[k] = first
        o2[k] = second
        for copy in out_copies(k)[:2]:
            copy.start()
        direction = (first / (jnp.sqrt(second) + EPSILON)).astype(BF)
        if k in (0, 2, 4):
            back[k, 0] = mm_t(direction, qr[k].reshape(512, 512)).astype(BF)
        if k in (1, 3, 4):
            back[k, 1] = mm_t(direction, qrs[(k - 1) // 2 if k < 4 else 2].reshape(512, 512)).astype(BF)

    def b_copy(p, dy):
        yy = lax.rem(y + dy, NY)
        return remote(bmsg.at[p, yy], bb.at[p, rep], s_b.at[p], r_b.at[p], (yy * 2 + PAIR_CORE[p], own))

    def send_back(p):
        a, b = PAIRS[p]
        for yy in range(NY):
            lanes = slice((yy // 2) * 128, (yy // 2) * 128 + 128)
            lo, hi = back[a, 0][:, lanes], back[b, 1][:, lanes]
            bmsg[p, yy] = jnp.where(lane_low, lo, hi) if yy % 2 == 0 else jnp.where(lane_low, hi, lo)
        for dy in far_first:
            b_copy(p, dy).start()

        @pl.when(c != PAIR_CORE[p])
        def _():
            b_copy(p, 0).start()

        @pl.when(c == PAIR_CORE[p])
        def _():
            bb[p, rep] = bmsg[p, y]

    def stat_products(k):
        @pl.when(active)
        def _():
            received(gall.at[k, pl.ds(0, NY - 1)], r_sib.at[k])

        for t in range(NY):
            gf[pl.ds((t // 4) * 256, 256), pl.ds((t % 4) * 128, 128)] = gall[k, t].reshape(256, 128)
        columns = mm_t(mine, gf[...]).astype(BF)
        right = mm(columns, gf[...])
        orr[k] = (BETA_SECOND * sr[k].astype(F32) + (1.0 - BETA_SECOND) * right).astype(BF)
        rows = mm(pm[pl.ds(pl.multiple_of(rep * 32, 32), 32), :], gf[...]).astype(BF)
        left = mm_t(mm_t(rows, gf[...]).astype(BF), pm[...])
        ol[k] = (BETA_SECOND * sl[k].astype(F32) + (1.0 - BETA_SECOND) * left).astype(BF)
        for copy in out_copies(k)[2:]:
            copy.start()

    def z2_copy(p, j):
        to = lax.rem(z + j, NZ)
        if p == 2:
            src, dst = ub4.at[to], w24.at[z]
        else:
            src, dst = ub.at[p, pl.ds(pl.multiple_of(to * 32, 32), 32)], w2.at[p, z]
        return remote(src, dst, s_z2.at[p], r_z2.at[p], at_z(to))

    def x2_copy(p, j, cc):
        to = lax.rem(x + j, NX)
        part = lax.rem(to, 2) if p == 2 else to
        return remote(xs2.at[p, part], yb.at[p, x], s_x2.at[p], r_x2.at[p], (y * 2 + cc, z * NX + to))

    def y_copy(p):
        return remote(yb.at[p], yb.at[p], s_y.at[p], r_y.at[p], sib)

    def update_products(p):
        received(bb.at[p, pl.ds(0, 15)], r_b.at[p])
        a, b = PAIRS[p]
        columns = bb[p].reshape(512, 128)
        if p == 2:
            whole = mm(ql[a], columns).astype(BF).reshape(NZ, 2, 16, 128)
            low = iota((NZ, 16, 128), 2) < 64
            ub4[...] = jnp.where(low, whole[:, 0], whole[:, 1])
        else:
            swap = jnp.where(iota((512, 128), 1) < 64, 0, 1) == (y & 1)
            ub[p] = jnp.where(swap, mm(ql[a], columns), mm(ql[b], columns)).astype(BF)
        for j in (8, 7, 9, 6, 10, 5, 11, 4, 12, 3, 13, 2, 14, 1, 15):
            z2_copy(p, j).start()
        if p == 2:
            w24[z] = ub4[z]
        else:
            w2[p, z] = ub[p, pl.ds(pl.multiple_of(z * 32, 32), 32)]

    def update_regroup(p):
        if p == 2:
            received(w24.at[pl.ds(0, NZ - 1)], r_z2.at[p])
            parts = mm(perm4[...], w24[...].reshape(256, 128)).astype(BF).reshape(2, 8, 16, 128)
            xs2[p, pl.ds(0, 2)] = parts
            for j in (2, 1, 3, 0):
                for cc in (1, 0)[: 1 + (j > 0)]:
                    x2_copy(p, j, cc).start()
            yb[p, x] = xs2[p, lax.rem(x, 2)]
        else:
            received(w2.at[p, pl.ds(0, NZ - 1)], r_z2.at[p])
            xs2[p] = mm(perm3[...], w2[p].reshape(512, 128)).astype(BF).reshape(NX, 8, 16, 128)
            for j in (2, 1, 3):
                x2_copy(p, j, PAIR_CORE[p]).start()
            yb[p, x] = xs2[p, x]

    def update_share(p):
        received(yb.at[p, pl.ds(0, NX - 1)], r_x2.at[p])
        if p != 2:
            y_copy(p).start()

    def on_core(core, step, p):
        @pl.when(c == core)
        def _():
            step(p)

    gather(0, (0, 1, 2))
    slot_products(0)
    gather(0, (3, 4))
    slot_products(1)
    send_back(0)
    slot_products(2)
    gather(1, (0, 1))
    slot_products(3)
    send_back(1)
    slot_products(4)
    send_back(2)
    gather(1, (2, 3, 4))
    j3 = iota((512, 1), 0)
    perm3[...] = onehot(iota((512, 512), 1), (j3 & 15) * 32 + (j3 >> 7) * 8 + ((j3 >> 4) & 7))
    perm4[...] = onehot(iota((256, 256), 1), (j2 & 15) * 16 + (j2 >> 7) * 8 + ((j2 >> 4) & 7))
    oh2[...] = onehot(iota((512, PADB), 0), slot_code)
    yb[pl.ds(3, 1)] = jnp.zeros((1, NX, 8, 16, 128), BF)
    on_core(0, update_products, 0)
    gather(2, (0, 1))
    on_core(1, update_products, 1)
    gather(2, (2,))
    on_core(0, update_products, 2)
    gather(2, (3, 4))
    gather(3, (0, 1, 2))
    on_core(0, update_regroup, 0)
    gather(3, (3, 4))
    gather(4, (0, 1))
    stat_products(0)
    gather(4, (2,))
    on_core(1, update_regroup, 1)
    gather(4, (3, 4))
    stat_products(1)
    on_core(0, update_share, 0)
    on_core(0, update_regroup, 2)
    stat_products(2)
    on_core(1, update_share, 1)
    stat_products(3)
    stat_products(4)

    chosen = onehot(
        iota((64, 128), 1), (iota((64, 1), 0) >> 5) * 64 + 32 * c + (iota((64, 1), 0) & 31)
    )

    def own_columns(first):
        for i in range(8):
            lanes = mm_t(chosen, yb[pl.ds(first, 2), :, i].reshape(128, 128)).astype(BF)
            wbuf[pl.ds(i * 32, 32), pl.ds(first * 64, 128)] = lanes[:32]
            wbuf[pl.ds(i * 32, 32), pl.ds(256 + first * 64, 128)] = lanes[32:]

    @pl.when(c == 0)
    def _():
        received(yb.at[1], r_y.at[1])

    @pl.when(c == 1)
    def _():
        received(yb.at[0], r_y.at[0])

    own_columns(0)

    @pl.when(c == 0)
    def _():
        update_share(2)

    @pl.when(c == 1)
    def _():
        received(yb.at[2], r_x2.at[2])

    own_columns(2)
    out_u[...] = mm(wbuf[...], oh2[...]).astype(BF)[:, :NB]

    def drain_4():
        @pl.when(active)
        def _():
            sent(hsend.at[:, pl.ds(0, 15)], s_h.at[0])
            sent(gall.at[:, 0], s_own.at[0])

        @pl.when(jnp.logical_not(active))
        def _():
            sent(gall.at[:, pl.ds(0, 7)], s_ag.at[0])
            sent(gall.at[:, pl.ds(0, 7)], s_sib.at[0])

        for p in range(3):

            @pl.when(c != PAIR_CORE[p])
            def _():
                sent(bmsg.at[p], s_b.at[p])

            @pl.when(c == PAIR_CORE[p])
            def _():
                sent(bmsg.at[p, pl.ds(0, 7)], s_b.at[p])
                if p == 2:
                    sent(ub4.at[pl.ds(0, NZ - 1)], s_z2.at[p])
                    sent(gall.at[0, pl.ds(0, 7), pl.ds(0, 2)], s_x2.at[p])
                else:
                    sent(w2.at[p, pl.ds(0, NZ - 1)], s_z2.at[p])
                    sent(yb.at[p, pl.ds(0, NX - 1)], s_x2.at[p])
                    sent(yb.at[p], s_y.at[p])

    drains.append(drain_4)
    for i, (src, dst) in enumerate(((o1, out_1), (o2, out_2), (ol, out_l), (orr, out_r))):
        pltpu.make_async_copy(src, dst, s_out.at[i]).wait()
    for drain in drains:
        drain()


def onehot_lt(a, b):
    return jnp.where(a < b, 1.0, 0.0).astype(BF)


def hand_on(*refs):
    sems = refs[-1]
    count = len(refs) // 2
    copies = [pltpu.make_async_copy(refs[i], refs[count + i], sems.at[i]) for i in range(count)]
    for copy in copies:
        copy.start()
    for copy in copies:
        copy.wait()


def shards(grad_parts, owner_of, stats_left, stats_right, basis_left, basis_right, moment_first, moment_second):
    blocks = owner_of.shape[0]
    anywhere = pl.BlockSpec(memory_space=pl.ANY)
    vmem = pl.BlockSpec(memory_space=pltpu.VMEM)
    rows = (SLOTS, 32, 512)
    dma = pltpu.SemaphoreType.DMA
    scratch = [
        pltpu.VMEM((1, PADB), jnp.int32),
        pltpu.VMEM((1152, 256), BF),
        pltpu.VMEM((1152, 256), BF),
        pltpu.VMEM((4, NB, 512), BF),
        pltpu.VMEM((2, 2, NB, 512), BF),
        pltpu.VMEM((2, 2, NB, 512), BF),
        pltpu.VMEM((2, NB, 512), BF),
        pltpu.VMEM((PADB, 512), BF),
        pltpu.VMEM((4, 640, PADB), BF),
        pltpu.VMEM((SLOTS, 8, 16, 128), BF),
        pltpu.VMEM((SLOTS, NZ, 16, 128), BF),
        pltpu.VMEM((SLOTS, NX, 4, 16, 128), BF),
        pltpu.VMEM((SLOTS, NY, 4, 64, 128), BF),
        pltpu.VMEM((SLOTS, 512, 512), BF),
        pltpu.VMEM((SLOTS, 4, 2, 64, 512), BF),
        pltpu.VMEM((3, 4, 2, 64, 512), BF),
        pltpu.VMEM(rows, BF),
        pltpu.VMEM(rows, BF),
        pltpu.VMEM(rows, F32),
        pltpu.VMEM(rows, F32),
        pltpu.VMEM(rows, BF),
        pltpu.VMEM(rows, BF),
        pltpu.VMEM(rows, F32),
        pltpu.VMEM(rows, F32),
        pltpu.VMEM((SLOTS, 512, 256), BF),
        pltpu.VMEM((SLOTS, 16, 32, 128), BF),
        pltpu.VMEM((SLOTS, NY, 32, 128), BF),
        pltpu.VMEM((512, 512), BF),
        pltpu.VMEM((512, 512), BF),
        pltpu.VMEM((256, 256), BF),
        pltpu.VMEM((512, 512), BF),
        pltpu.VMEM((256, 256), BF),
        pltpu.VMEM((512, PADB), BF),
        pltpu.VMEM((256, 512), BF),
        pltpu.VMEM((3, NY, 32, 128), BF),
        pltpu.VMEM((3, 16, 32, 128), BF),
        pltpu.VMEM((2, 512, 128), BF),
        pltpu.VMEM((NZ, 16, 128), BF),
        pltpu.VMEM((2, NZ, 32, 128), BF),
        pltpu.VMEM((NZ, 16, 128), BF),
        pltpu.VMEM((3, NX, 8, 16, 128), BF),
        pltpu.VMEM((4, NX, 8, 16, 128), BF),
        dma((8,)),
        dma((4,)),
        dma((1,)), dma((3,)),
        dma((1,)), dma((2, 2, SUBS)), dma((SUBS,)),
        dma((1,)), dma((1,)),
        dma((1,)), dma((SLOTS,)),
        dma((1,)), dma((SLOTS,)),
        dma((1,)), dma((SLOTS,)),
        dma((1,)), dma((SLOTS,)),
        dma((1,)), dma((2, 4, SLOTS)),
        dma((1,)), dma((SLOTS,)),
        dma((3,)), dma((3,)),
        dma((3,)), dma((3,)),
        dma((3,)), dma((3,)),
        dma((2,)), dma((2,)),
    ]
    shapes = (
        jax.ShapeDtypeStruct(rows, BF),
        jax.ShapeDtypeStruct(rows, BF),
        jax.ShapeDtypeStruct(rows, F32),
        jax.ShapeDtypeStruct(rows, F32),
        jax.ShapeDtypeStruct((256, blocks), BF),
    )
    results = pl.pallas_call(
        kernel,
        out_shape=shapes,
        in_specs=[anywhere, vmem] + [anywhere] * 6,
        out_specs=(anywhere,) * 4 + (vmem,),
        scratch_shapes=scratch,
        compiler_params=pltpu.CompilerParams(
            collective_id=0, has_side_effects=True, vmem_limit_bytes=56 * 1024 * 1024
        ),
    )(
        grad_parts[0].reshape(blocks * 8, 512),
        owner_of.reshape(1, blocks),
        stats_left[0],
        stats_right[0],
        basis_left[0],
        basis_right[0].reshape(SLOTS, 4, 2, 64, 512),
        moment_first[0],
        moment_second[0],
    )
    new_left, new_right, new_first, new_second, picked = pl.pallas_call(
        hand_on,
        out_shape=shapes,
        in_specs=[vmem] * 5,
        out_specs=(anywhere,) * 5,
        scratch_shapes=[dma((5,))],
    )(*results)
    update = picked.reshape(8, 32, blocks).transpose(2, 0, 1)
    return (new_left[None], new_right[None], new_first[None], new_second[None], update)


def solution(mesh):
    return jax.shard_map(
        shards,
        mesh=mesh,
        in_specs=(
            P("replica", None, "owner", None),
            P(),
            P("owner", None, "replica", None),
            P("owner", None, "replica", None),
            P("owner", None, None, None),
            P("owner", None, None, None),
            P("owner", None, "replica", None),
            P("owner", None, "replica", None),
        ),
        out_specs=(
            P("owner", None, "replica", None),
            P("owner", None, "replica", None),
            P("owner", None, "replica", None),
            P("owner", None, "replica", None),
            P(None, "owner", "replica"),
        ),
        check_vma=False,
    )
```
